128 devices in a mesh: pb: 4 (over z), al: 32 (over x, y, core).
Axes of the slice: x: 4, y: 4, z: 4, core: 2. Of those that a mesh axis runs over, the one named last changes fastest.
Arguments:
- queries: bfloat16 [32768, 768], P(('pb', 'al')), may hold values from -6 to 6
- classifier: float32 [1024, 128, 768], P('al'), may hold values from -0.21875 to 0.21875
- routed: int32 [32768, 16], P(('pb', 'al')), may hold values from 0 to 1023, all different within a row; in each aligned block of 256 rows (0 to 255, 256 to 511, ...) at most 10 rows name the same one
- positives: int32 [32768, 16], P(('pb', 'al')), may hold values from 0 to 255
- cluster_slot: int32 [1024], replicated, may hold values from 0 to 1023, each once
Outputs:
- query_grad: float32 [32768, 768], P(('pb', 'al'))
- class_grad: float32 [1024, 128, 768], P('al', 'pb')
The draws below stay inside these ranges and needn't reach their ends.
Inputs may be any that keep to these rules, and one draw needn't show every extreme that they name: `routed`: each row names 16 distinct clusters; among the rows of one device no cluster is named more than 10 times, a bound that some block reaches. `positives`: a value v below 128 names leaf v of the cluster in the same column of routed as positive; larger values name none. `cluster_slot`: each slot once.
All inputs are finite; a program needn't handle non-finite values.
Results may differ from the reference program's by a relative error of at most 0.012.
Values may be sent and summed in bfloat16 or wider, within the bound.
No kernel may reach another device: no remote copies, remote signals or barrier semaphores. Data moves between devices by JAX's collectives and lax.ppermute only.
A program may use at most 192 MiB of HBM per device.

```python
import math
import jax
import jax.numpy as jnp
import numpy as np
from jax import lax

D = 768
LEAF = 128
TOP = 16
Q_DEV = 256
CLUSTERS = 1024
QUERIES = 32768
CAP = 10
N_PB = 4
N_AL = 32


def with_ends(values, key, smallest, high):
    index_at = [jax.random.randint(jax.random.fold_in(key, axis), (), 0, length) for axis, length in enumerate(values.shape)]
    main_axis = values.shape.index(max(values.shape))
    beside = index_at[:main_axis] + [(index_at[main_axis] + 1) % values.shape[main_axis]] + index_at[main_axis + 1:]
    return values.at[tuple(index_at)].set(smallest).at[tuple(beside)].set(high)


def steps_of(own_key, shape, split, least, largest):
    def one(position, parts):
        heights = jax.random.uniform(jax.random.fold_in(jax.random.fold_in(own_key, 6), position), (parts,), jnp.float32, least / len(split), largest / len(split))
        return jnp.repeat(jnp.exp(heights), shape[position] // parts).reshape((-1,) + (1,) * (len(shape) - position - 1))

    loudness = one(*split[0])
    for cut in split[1:]:
        loudness = loudness * one(*cut)
    return loudness


def deal_out(rng, own, number, rows, count, top, bound, lean):
    ranking = jax.random.permutation(rng, count)
    crowded, common = load_shares(count, rows * top, bound, lean, True), load_shares(count, rows * top, bound, lean, False)
    places = jnp.arange(count)

    def named(tallies, rotation):
        used = int((tallies > 0).sum())
        fixed = max(1, used // 4)
        shifted = fixed + (places - fixed + rotation * (used - fixed)) % max(1, count - fixed)
        return jnp.zeros((count,), jnp.int32).at[ranking[jnp.where(places < fixed, places, shifted)]].set(jnp.asarray(tallies, jnp.int32))

    tallies = jnp.where(number % 4 == 0, named(crowded, number // 4), named(common, number - number // 4 - 1))
    mixed = jax.random.permutation(jax.random.fold_in(own, 3), count)
    donor, sink = mixed[0:count // 2 * 2:2], mixed[1:count // 2 * 2:2]
    margin = jnp.minimum(tallies[donor] - 1, bound - tallies[sink]) // 2
    margin = jnp.where((donor == ranking[0]) | (sink == ranking[0]) | (tallies[sink] == 0), 0, jnp.maximum(margin, 0))
    shifted = jax.random.randint(jax.random.fold_in(own, 4), (count // 2,), 0, 1 << 20) % (margin + 1)
    tallies = tallies.at[donor].add(-shifted).at[sink].add(shifted)
    items = jnp.searchsorted(jnp.cumsum(tallies), jnp.arange(rows * top), side="right").astype(jnp.int32)
    table = items.reshape(top, rows).T
    table = table[jax.random.permutation(jax.random.fold_in(own, 1), rows)]
    rotation = jax.random.randint(jax.random.fold_in(own, 2), (rows, 1), 0, top)
    return jnp.take_along_axis(table, (jnp.arange(top)[None, :] + rotation) % top, axis=1)


def load_shares(count, total, bound, skew, full):
    portions = [(1 << 20) // math.isqrt(standing ** skew) + 1 for standing in range(1, count + 1)]
    largest = bound if full else min(bound, max(-(-total // count), total * portions[0] // sum(portions)))
    least = 1 if total - largest >= count - 1 else 0
    counts, surplus = [largest] + [least] * (count - 1), total - largest - least * (count - 1)
    while surplus > 0:
        movable = [i for i in range(1, count) if counts[i] < largest] or [i for i in range(1, count) if counts[i] < bound]
        pool, budget = sum([portions[i] for i in movable]), surplus
        for i in movable:
            extra = min(bound - counts[i], max(1, budget * portions[i] // pool), surplus)
            counts[i] = counts[i] + extra
            surplus = surplus - extra
    return np.array(counts)


def noise(own_key, dims, spread, bound, shards=(), kind=jnp.bfloat16):
    values = jax.random.normal(own_key, dims, jnp.float32) * spread
    if len(shards) > 0:
        values = steps_of(own_key, dims, shards, -0.22, 0.18) * values
    return jnp.clip(values, min=-bound, max=bound).astype(kind)


def setup_inputs(seed: int = 0) -> dict:
    key_of = jax.random.split(jax.random.key(seed), 6)
    queries = noise(key_of[0], (QUERIES, D), 1.0, 6.0, ((0, 128),))
    classifier = noise(key_of[1], (CLUSTERS, LEAF, D), D ** -0.5, 0.21875, ((0, 32),), jnp.float32)
    routed_keys = jax.random.split(jax.random.fold_in(key_of[2], 1), QUERIES // Q_DEV)
    routed_turns = jax.random.permutation(jax.random.fold_in(key_of[2], 3), QUERIES // Q_DEV)
    routed = jax.vmap(lambda own, number: deal_out(jax.random.fold_in(key_of[2], 2), own, number, Q_DEV, CLUSTERS, TOP, CAP, 2))(routed_keys, routed_turns).reshape((QUERIES, TOP))
    positives = with_ends(jax.random.randint(key_of[3], (QUERIES, TOP), 0, 2 * LEAF), jax.random.fold_in(key_of[3], 1), 0, (2 * LEAF) - 1).astype(jnp.int32)
    cluster_slot = jax.random.permutation(key_of[4], CLUSTERS).astype(jnp.int32)
    return {"queries": queries, "classifier": classifier, "routed": routed, "positives": positives, "cluster_slot": cluster_slot}


def ranks_of(flattened):
    order = jnp.argsort(flattened, stable=True)
    ordered = flattened[order]
    first = jnp.searchsorted(ordered, ordered, side="left").astype(jnp.int32)
    place = jnp.arange(flattened.shape[0], dtype=jnp.int32) - first
    return jnp.zeros_like(flattened).at[order].set(place)


def reference(queries, classifier, routed, positives, cluster_slot):
    devices = N_PB * N_AL
    pairs = Q_DEV * TOP
    route_dev = routed.reshape(devices, pairs)
    rank_ids = jax.vmap(ranks_of)(route_dev)
    slot_ids = cluster_slot[route_dev]
    device_ids = jnp.arange(devices, dtype=jnp.int32)
    group_ids = (device_ids // N_AL)[:, None]
    source_ids = (device_ids % N_AL)[:, None]
    query_ids = device_ids[:, None] * Q_DEV + jnp.arange(pairs, dtype=jnp.int32)[None, :] // TOP
    table = jnp.full((N_PB, CLUSTERS, N_AL, CAP), QUERIES, jnp.int32)
    table = table.at[group_ids, slot_ids, source_ids, rank_ids].set(query_ids)
    target = jnp.full((N_PB, CLUSTERS, N_AL, CAP), -1, jnp.int32)
    target = target.at[group_ids, slot_ids, source_ids, rank_ids].set(positives.reshape(devices, pairs))
    weights = classifier.astype(jnp.bfloat16)
    padded = jnp.concatenate([queries, jnp.zeros((1, D), jnp.bfloat16)], axis=0)
    leaf_ids = jnp.arange(LEAF, dtype=jnp.int32)

    def visit(carry, cluster):
        rows = table[:, cluster].reshape(-1)
        wanted = target[:, cluster].reshape(-1)
        gathered = padded[rows]
        weight = weights[cluster]
        logits = jnp.dot(gathered, weight.T, preferred_element_type=jnp.float32)
        labels = (wanted[:, None] == leaf_ids[None, :]).astype(jnp.float32)
        residual = jnp.where((wanted >= 0)[:, None], jax.nn.sigmoid(logits) - labels, jnp.float32(0.0))
        residual = residual.astype(jnp.bfloat16)
        pair_grad = jnp.dot(residual, weight, preferred_element_type=jnp.float32).astype(jnp.bfloat16)
        carry = carry.at[rows].add(pair_grad.astype(jnp.float32), mode="drop")
        res_group = residual.reshape(N_PB, N_AL * CAP, LEAF).astype(jnp.float32)
        row_group = gathered.reshape(N_PB, N_AL * CAP, D).astype(jnp.float32)
        group_grad = jnp.einsum("prc,prd->pcd", res_group, row_group).astype(jnp.bfloat16)
        group_grad = lax.optimization_barrier(group_grad)
        return carry, jnp.sum(group_grad.astype(jnp.float32), axis=0)

    start = jnp.zeros((QUERIES, D), jnp.float32)
    query_grad, class_grad = lax.scan(visit, start, jnp.arange(CLUSTERS, dtype=jnp.int32))
    return query_grad, class_grad
```

```python
import functools

import jax
import jax.numpy as jnp
from jax import lax
from jax.experimental import pallas as pl
from jax.experimental.pallas import tpu as pltpu
from jax.sharding import PartitionSpec as P

F32 = jnp.float32
BF16 = jnp.bfloat16
SIDE = 4
QUERIES = 256
TOP = 16
WIDTH = 768
LEAF = 128
LOCAL = 32
SOURCES = 8
HALF = 4
ROWS = 80
PAYLOAD = QUERIES + TOP
CHUNK = HALF * QUERIES
BLOCK = HALF * PAYLOAD
MIB = 1 << 20


def al_index(x, y, core):
    return ((x % SIDE) * SIDE + y % SIDE) * 2 + core


def shift(first, second):
    pairs = []
    for x in range(SIDE):
        for y in range(SIDE):
            pairs.append((al_index(x, y, 0), al_index(x + first[0], y + first[1], 0)))
            pairs.append((al_index(x, y, 1), al_index(x + second[0], y + second[1], 1)))
    return pairs


NEAR_UP, NEAR_DOWN = shift((1, 0), (0, 1)), shift((-1, 0), (0, -1))
FAR_UP, FAR_DOWN = shift((0, 1), (1, 0)), shift((0, -1), (-1, 0))
SWAP = [(i, i ^ 1) for i in range(2 * SIDE * SIDE)]
Z_UP = [(i, (i + 1) % SIDE) for i in range(SIDE)]
Z_DOWN = [(i, (i - 1) % SIDE) for i in range(SIDE)]


def send(value, pairs):
    return lax.ppermute(value, "al", pairs)


def send_z(value, pairs):
    return lax.ppermute(value, "pb", pairs)


def add(first, *others):
    total = first.astype(F32)
    for other in others:
        total = total + other.astype(F32)
    return total


def routing_block(routed, positives, cluster_slot):
    ids = routed.T.reshape(-1)
    table = cluster_slot.reshape(32, 32).T
    table = jnp.concatenate([table // LOCAL, table % LOCAL], axis=0).astype(BF16)
    digit = jnp.arange(32, dtype=jnp.int32)[:, None]
    high = (ids[None, :] // 32 == digit).astype(BF16)
    picked = jnp.dot(table, high, preferred_element_type=F32).reshape(2, 32, TOP, QUERIES)
    low = (ids[None, :] % 32 == digit).reshape(32, TOP, QUERIES)
    owner_local = jnp.sum(jnp.where(low[None], picked, 0.0), axis=1).astype(BF16)
    return jnp.concatenate([owner_local[0], owner_local[1], positives.T.astype(BF16)], axis=1)


def chunk_kernel(pieces, me_ref, *refs):
    parts = refs[: len(pieces)]
    w_ref, x_ref, r_ref, own_ref, sibling_ref, q_ref, target_ref, grad_ref, rank_ref, sems = refs[
        len(pieces) :
    ]
    copies = []
    for n, (part, (side, start, count)) in enumerate(zip(parts, pieces)):
        copy = pltpu.make_async_copy(part, q_ref.at[side, pl.ds(start, count)], sems.at[n])
        copy.start()
        copies.append(copy)
    for copy in copies:
        copy.wait()
    me = me_ref[0].astype(F32)
    before = (
        lax.broadcasted_iota(jnp.int32, (QUERIES, QUERIES), 0)
        < lax.broadcasted_iota(jnp.int32, (QUERIES, QUERIES), 1)
    ).astype(BF16)
    clusters = lax.broadcasted_iota(jnp.int32, (LOCAL, QUERIES), 0).astype(F32)
    places = lax.broadcasted_iota(jnp.int32, (LOCAL, 8, QUERIES), 1).astype(F32)
    ones = jnp.ones((QUERIES, LEAF), BF16)

    def spread(value):
        return jnp.broadcast_to(value[:, None, :], (LOCAL, 8, QUERIES))

    def source(s):
        return s // HALF, s % HALF

    def queries_of(s):
        side, i = source(s)
        return q_ref[side, i * QUERIES : (i + 1) * QUERIES, :]

    rows = [None] * SOURCES
    for side in range(2):
        extra = []
        extra_target = []
        for i in range(HALF):
            s = side * HALF + i
            start = CHUNK + i * TOP
            meta = q_ref[side, start : start + TOP, :].astype(F32)
            key = jnp.where(meta[:, :QUERIES] == me, meta[:, QUERIES : 2 * QUERIES], -1.0)
            code = jnp.zeros((LOCAL, QUERIES), F32)
            for j in range(TOP):
                label = meta[j : j + 1, 2 * QUERIES :] + 1.0
                code = code + jnp.where(key[j : j + 1, :] == clusters, label, 0.0)
            filled = code > 0.0
            rank = jnp.dot(filled.astype(BF16), before, preferred_element_type=F32)
            rank = jnp.where(filled, rank, -1.0)
            rank_ref[s] = rank
            match = spread(rank) == places
            code_rows = spread(code)
            pick = match.astype(BF16).reshape(LOCAL * 8, QUERIES)
            labels = jnp.where(match, code_rows, 0.0).astype(BF16).reshape(LOCAL * 8, QUERIES)
            rows[s] = jnp.dot(pick, queries_of(s), preferred_element_type=F32).reshape(
                LOCAL, 8, WIDTH
            )
            target_ref[:, s * 8 : s * 8 + 8, :] = jnp.dot(
                labels, ones, preferred_element_type=F32
            ).reshape(LOCAL, 8, LEAF)
            late = jnp.where(rank >= 8.0, rank - 8.0 + 2.0 * i, -1.0)
            match = spread(late) == places
            extra.append(match.astype(BF16).reshape(LOCAL * 8, QUERIES))
            extra_target.append(
                jnp.where(match, code_rows, 0.0).astype(BF16).reshape(LOCAL * 8, QUERIES)
            )
            if i % 2 == 1:
                pair = jnp.concatenate([rows[s - 1], rows[s]], axis=1).astype(BF16)
                x_ref[:, (s - 1) * 8 : (s + 1) * 8, :] = pair
        late_rows = jnp.dot(
            jnp.concatenate(extra, axis=1), q_ref[side, :CHUNK, :], preferred_element_type=F32
        ).reshape(LOCAL, 8, WIDTH)
        late_labels = sum(jnp.dot(e, ones, preferred_element_type=F32) for e in extra_target)
        target_ref[:, 64 + side * 8 : 72 + side * 8, :] = late_labels.reshape(LOCAL, 8, LEAF)
        if side == 0:
            first_late = late_rows
        else:
            x_ref[:, 64:80, :] = jnp.concatenate([first_late, late_rows], axis=1).astype(BF16)

    leaves = lax.broadcasted_iota(jnp.int32, (ROWS, LEAF), 1).astype(F32) + 1.0

    @pl.loop(0, LOCAL)
    def _(c):
        weight = w_ref[c]
        logits = lax.dot_general(
            x_ref[c], weight, (((1,), (1,)), ((), ())), preferred_element_type=F32
        )
        label = (target_ref[c] == leaves).astype(F32)
        residual = (jax.nn.sigmoid(logits) - label).astype(BF16)
        r_ref[c] = residual
        grad_ref[c] = jnp.dot(residual, weight, preferred_element_type=F32)

    for s in range(SOURCES):
        side, i = source(s)
        rank = rank_ref[s]
        pick = (spread(rank) == places).astype(BF16).reshape(LOCAL * 8, QUERIES)
        late = jnp.where(rank >= 8.0, rank - 8.0 + 2.0 * i, -1.0)
        late_pick = (spread(late) == places).astype(BF16).reshape(LOCAL * 8, QUERIES)
        picks = jnp.concatenate([pick, late_pick], axis=0)
        near = grad_ref[:, s * 8 : s * 8 + 8, :].reshape(LOCAL * 8, WIDTH).astype(BF16)
        far = grad_ref[:, 64 + side * 8 : 72 + side * 8, :].reshape(LOCAL * 8, WIDTH).astype(BF16)
        total = lax.dot_general(
            picks,
            jnp.concatenate([near, far], axis=0),
            (((0,), (0,)), ((), ())),
            preferred_element_type=F32,
        ).astype(BF16)
        out = sibling_ref if side else own_ref
        out[i * QUERIES : (i + 1) * QUERIES, :] = total


def chunk(me, parts, weights):
    pieces = [(side, start, part.shape[0]) for part, side, start in parts]
    anywhere = pl.BlockSpec(memory_space=pl.ANY)
    in_vmem = pl.BlockSpec(memory_space=pltpu.VMEM)
    return pl.pallas_call(
        functools.partial(chunk_kernel, pieces),
        out_shape=(
            jax.ShapeDtypeStruct((LOCAL, ROWS, WIDTH), BF16),
            jax.ShapeDtypeStruct((LOCAL, ROWS, LEAF), BF16),
            jax.ShapeDtypeStruct((CHUNK, WIDTH), BF16),
            jax.ShapeDtypeStruct((CHUNK, WIDTH), BF16),
        ),
        in_specs=[pl.BlockSpec(memory_space=pltpu.SMEM)] + [anywhere] * len(parts) + [in_vmem],
        out_specs=(in_vmem,) * 4,
        scratch_shapes=[
            pltpu.VMEM((2, BLOCK, WIDTH), BF16),
            pltpu.VMEM((LOCAL, ROWS, LEAF), F32),
            pltpu.VMEM((LOCAL, ROWS, WIDTH), F32),
            pltpu.VMEM((SOURCES, LOCAL, QUERIES), F32),
            pltpu.SemaphoreType.DMA((len(parts),)),
        ],
        compiler_params=pltpu.CompilerParams(vmem_limit_bytes=48 * MIB),
        cost_estimate=pl.CostEstimate(
            flops=8 * 10**9, bytes_accessed=20 * 10**6, transcendentals=0
        ),
    )(me, *[part for part, _, _ in parts], weights)


def class_kernel(group_ref, *refs):
    xs, rs, outs = refs[:4], refs[4:8], refs[8:12]
    x_buf, r_buf, total_ref = refs[12:]
    group = group_ref[0]
    step = xs[0].shape[0]
    for c in range(step):
        for n in range(4):
            x_buf[n * ROWS : (n + 1) * ROWS, :] = xs[n][c]
            r_buf[n * ROWS : (n + 1) * ROWS, :] = rs[n][c]
        total_ref[...] = lax.dot_general(
            r_buf[...], x_buf[...], (((0,), (0,)), ((), ())), preferred_element_type=F32
        )
        for n in range(4):
            start = pl.multiple_of(((group + n) % 4) * 32, 32)
            outs[n][c] = total_ref[pl.ds(start, 32), :].astype(BF16)


def class_grads(group, xs, rs):
    step = 4

    def spec(rows, width):
        return pl.BlockSpec((step, rows, width), lambda c: (c, 0, 0))

    return pl.pallas_call(
        class_kernel,
        grid=(LOCAL // step,),
        out_shape=(jax.ShapeDtypeStruct((LOCAL, 32, WIDTH), BF16),) * 4,
        in_specs=[pl.BlockSpec(memory_space=pltpu.SMEM)]
        + [spec(ROWS, WIDTH)] * 4
        + [spec(ROWS, LEAF)] * 4,
        out_specs=(spec(32, WIDTH),) * 4,
        scratch_shapes=[
            pltpu.VMEM((4 * ROWS, WIDTH), BF16),
            pltpu.VMEM((4 * ROWS, LEAF), BF16),
            pltpu.VMEM((LEAF, WIDTH), F32),
        ],
        compiler_params=pltpu.CompilerParams(vmem_limit_bytes=40 * MIB),
        cost_estimate=pl.CostEstimate(
            flops=4 * 10**9, bytes_accessed=25 * 10**6, transcendentals=0
        ),
    )(group, *xs, *rs)


def body(queries, classifier, routed, positives, cluster_slot):
    weights = classifier.astype(BF16)
    me = lax.axis_index("al").astype(jnp.int32).reshape(1)
    group = lax.axis_index("pb").astype(jnp.int32).reshape(1)
    payload = jnp.concatenate([queries, routing_block(routed, positives, cluster_slot)], axis=0)

    up, down = send(payload, NEAR_UP), send(payload, NEAR_DOWN)
    cut = 144
    across_a, across_b = send(up[:cut], NEAR_UP), send(down[cut:], NEAR_DOWN)
    across = jnp.concatenate([across_a, across_b], axis=0)
    near = [payload, up, down, across]
    home = jnp.concatenate([p[:QUERIES] for p in near] + [p[QUERIES:] for p in near], axis=0)
    far_up, far_down = send(home, FAR_UP), send(home, FAR_DOWN)
    mid = BLOCK // 2
    far_a, far_b = send(far_up[:mid], FAR_UP), send(far_down[mid:], FAR_DOWN)

    def both(arrays):
        parts, start = [], 0
        for array in arrays:
            parts += [(array, 0, start), (send(array, SWAP), 1, start)]
            start += array.shape[0]
        return parts

    results = [
        chunk(me, both(arrays), weights)
        for arrays in ([home], [far_up], [far_down], [far_a, far_b])
    ]
    xs, rs = [r[0] for r in results], [r[1] for r in results]

    own, next_up, opposite, next_down = class_grads(group, xs, rs)
    cut = LOCAL // 2
    hop_up, hop_down = send_z(opposite[:cut], Z_UP), send_z(opposite[cut:], Z_DOWN)
    from_down_b = send_z(next_up[cut:], Z_UP)
    from_up_a = send_z(next_down[:cut], Z_DOWN)
    from_down_a = send_z(add(next_up[:cut], hop_up).astype(BF16), Z_UP)
    from_up_b = send_z(add(next_down[cut:], hop_down).astype(BF16), Z_DOWN)
    class_grad = jnp.concatenate(
        [add(own[:cut], from_down_a, from_up_a), add(own[cut:], from_down_b, from_up_b)], axis=0
    )

    home, far_up, far_down, opposite = [
        add(r[2], send(r[3], SWAP)).astype(BF16) for r in results
    ]

    def scatter(up_part, down_part, opposite_part, up_pairs, down_pairs):
        cut = opposite_part.shape[0] // 2
        hop_up, hop_down = send(opposite_part[:cut], up_pairs), send(opposite_part[cut:], down_pairs)
        low_b = send(down_part[cut:], up_pairs)
        high_a = send(up_part[:cut], down_pairs)
        low_a = send(add(down_part[:cut], hop_up).astype(BF16), up_pairs)
        high_b = send(add(up_part[cut:], hop_down).astype(BF16), down_pairs)
        return (low_a, low_b), (high_a, high_b)

    low, high = scatter(far_up, far_down, opposite, FAR_UP, FAR_DOWN)
    mid = CHUNK // 2
    total = jnp.concatenate([add(home[:mid], low[0], high[0]), add(home[mid:], low[1], high[1])])
    mine, up, down, across = [
        total[i * QUERIES : (i + 1) * QUERIES] for i in range(HALF)
    ]
    low, high = scatter(
        up.astype(BF16), down.astype(BF16), across.astype(BF16), NEAR_UP, NEAR_DOWN
    )
    mid = QUERIES // 2
    query_grad = jnp.concatenate(
        [add(mine[:mid], low[0], high[0]), add(mine[mid:], low[1], high[1])], axis=0
    )
    return query_grad, class_grad


def solution(mesh):
    return jax.shard_map(
        body,
        mesh=mesh,
        in_specs=(
            P(("pb", "al"), None),
            P("al", None, None),
            P(("pb", "al"), None),
            P(("pb", "al"), None),
            P(),
        ),
        out_specs=(P(("pb", "al"), None), P("al", "pb", None)),
        check_vma=False,
    )
```

```python
import functools

import jax
import jax.numpy as jnp
from jax import lax
from jax.experimental import pallas as pl
from jax.experimental.pallas import tpu as pltpu
from jax.sharding import PartitionSpec as P

F32 = jnp.float32
BF16 = jnp.bfloat16
SIDE = 4
QUERIES = 256
TOP = 16
WIDTH = 768
LEAF = 128
LOCAL = 32
SOURCES = 8
HALF = 4
ROWS = 80
PAYLOAD = QUERIES + TOP
CHUNK = HALF * QUERIES
STACK = 2 * PAYLOAD
MIB = 1 << 20
UNROLL = 8


def al_index(x, y, core):
    return ((x % SIDE) * SIDE + y % SIDE) * 2 + core


def shift(first, second):
    pairs = []
    for x in range(SIDE):
        for y in range(SIDE):
            pairs.append((al_index(x, y, 0), al_index(x + first[0], y + first[1], 0)))
            pairs.append((al_index(x, y, 1), al_index(x + second[0], y + second[1], 1)))
    return pairs


NEAR_UP, NEAR_DOWN = shift((1, 0), (0, 1)), shift((-1, 0), (0, -1))
FAR_UP, FAR_DOWN = shift((0, 1), (1, 0)), shift((0, -1), (-1, 0))
SWAP = [(i, i ^ 1) for i in range(2 * SIDE * SIDE)]
Z_UP = [(i, (i + 1) % SIDE) for i in range(SIDE)]
Z_DOWN = [(i, (i - 1) % SIDE) for i in range(SIDE)]


def send(value, pairs):
    return lax.ppermute(value, "al", pairs)


def send_z(value, pairs):
    return lax.ppermute(value, "pb", pairs)


def add(first, *others):
    total = first.astype(F32)
    for other in others:
        total = total + other.astype(F32)
    return total


def payload_kernel(q_ref, routed_ref, positives_ref, table_ref, out_ref):
    out_ref[:QUERIES, :] = q_ref[...]
    slots = table_ref[...]
    table = jnp.concatenate([slots // LOCAL, slots % LOCAL], axis=0).astype(F32).astype(BF16)
    lanes = lax.broadcasted_iota(jnp.int32, (128, QUERIES), 0)
    highs = lax.broadcasted_iota(jnp.int32, (8, QUERIES), 0)
    ids = routed_ref[...]
    rows = []
    for j in range(TOP):
        one = ids[j : j + 1, :]
        low = (one % 128 == lanes).astype(F32).astype(BF16)
        found = jnp.dot(table, low, preferred_element_type=F32)
        high = one // 128 == highs
        rows.append(
            jnp.concatenate(
                [
                    jnp.sum(jnp.where(high, found[:8], 0.0), axis=0, keepdims=True),
                    jnp.sum(jnp.where(high, found[8:], 0.0), axis=0, keepdims=True),
                ],
                axis=1,
            )
        )
    found = jnp.concatenate(rows, axis=0)
    labels = positives_ref[...].astype(F32)
    out_ref[QUERIES:, :] = jnp.concatenate([found, labels], axis=1).astype(BF16)


def payload_of(queries, routed, positives, cluster_slot):
    return pl.pallas_call(
        payload_kernel,
        out_shape=jax.ShapeDtypeStruct((PAYLOAD, WIDTH), BF16),
        cost_estimate=pl.CostEstimate(flops=10**8, bytes_accessed=10**6, transcendentals=0),
    )(queries, routed.T, positives.T, cluster_slot.reshape(8, 128))


def chunk_kernel(me_ref, *refs):
    stacks, (w_hbm, x_hbm, r_hbm, own_hbm, sibling_hbm) = refs[:4], refs[4:9]
    q_ref, w_ref, x_ref, r_ref, p_ref, target_ref, grad_ref, rank_ref, sems = refs[9:]
    copies = [
        pltpu.make_async_copy(stack, q_ref.at[n], sems.at[n]) for n, stack in enumerate(stacks)
    ]
    weights_copy = pltpu.make_async_copy(w_hbm, w_ref, sems.at[4])
    for copy in copies + [weights_copy]:
        copy.start()
    x_copy = pltpu.make_async_copy(x_ref, x_hbm, sems.at[5])
    r_copy = pltpu.make_async_copy(r_ref, r_hbm, sems.at[6])
    p_copies = [
        pltpu.make_async_copy(p_ref.at[side], out, sems.at[7 + side])
        for side, out in enumerate((own_hbm, sibling_hbm))
    ]
    me = me_ref[0].astype(F32)
    before = (
        lax.broadcasted_iota(jnp.int32, (QUERIES, QUERIES), 0)
        < lax.broadcasted_iota(jnp.int32, (QUERIES, QUERIES), 1)
    ).astype(BF16)
    clusters = lax.broadcasted_iota(jnp.int32, (LOCAL, QUERIES), 0).astype(F32)
    places = lax.broadcasted_iota(jnp.int32, (LOCAL, 8, QUERIES), 1).astype(F32)
    ones = jnp.ones((QUERIES, LEAF), BF16)

    def spread(value):
        return jnp.broadcast_to(value[:, None, :], (LOCAL, 8, QUERIES))

    def source(s):
        return s // HALF, s % HALF

    def queries_of(s):
        return q_ref[s // 2, s % 2 * QUERIES : (s % 2 + 1) * QUERIES, :]

    rows = [None] * SOURCES
    for side in range(2):
        extra = []
        extra_target = []
        for i in range(HALF):
            s = side * HALF + i
            if s % 2 == 0:
                copies[s // 2].wait()
            start = 2 * QUERIES + s % 2 * TOP
            meta = q_ref[s // 2, start : start + TOP, :].astype(F32)
            key = jnp.where(meta[:, :QUERIES] == me, meta[:, QUERIES : 2 * QUERIES], -1.0)
            code = jnp.zeros((LOCAL, QUERIES), F32)
            for j in range(TOP):
                label = meta[j : j + 1, 2 * QUERIES :] + 1.0
                code = code + jnp.where(key[j : j + 1, :] == clusters, label, 0.0)
            filled = code > 0.0
            rank = jnp.dot(filled.astype(BF16), before, preferred_element_type=F32)
            rank = jnp.where(filled, rank, -1.0)
            rank_ref[s] = rank
            match = spread(rank) == places
            code_rows = spread(code)
            pick = match.astype(BF16).reshape(LOCAL * 8, QUERIES)
            labels = jnp.where(match, code_rows, 0.0).astype(BF16).reshape(LOCAL * 8, QUERIES)
            rows[s] = jnp.dot(pick, queries_of(s), preferred_element_type=F32).reshape(
                LOCAL, 8, WIDTH
            )
            target_ref[:, s * 8 : s * 8 + 8, :] = jnp.dot(
                labels, ones, preferred_element_type=F32
            ).reshape(LOCAL, 8, LEAF)
            late = jnp.where(rank >= 8.0, rank - 8.0 + 2.0 * i, -1.0)
            match = spread(late) == places
            extra.append(match.astype(BF16).reshape(LOCAL * 8, QUERIES))
            extra_target.append(
                jnp.where(match, code_rows, 0.0).astype(BF16).reshape(LOCAL * 8, QUERIES)
            )
            if i % 2 == 1:
                pair = jnp.concatenate([rows[s - 1], rows[s]], axis=1).astype(BF16)
                x_ref[:, (s - 1) * 8 : (s + 1) * 8, :] = pair
        late_rows = sum(
            jnp.dot(
                jnp.concatenate(extra[2 * n : 2 * n + 2], axis=1),
                q_ref[2 * side + n, : 2 * QUERIES, :],
                preferred_element_type=F32,
            )
            for n in range(2)
        ).reshape(LOCAL, 8, WIDTH)
        late_labels = sum(jnp.dot(e, ones, preferred_element_type=F32) for e in extra_target)
        target_ref[:, 64 + side * 8 : 72 + side * 8, :] = late_labels.reshape(LOCAL, 8, LEAF)
        if side == 0:
            first_late = late_rows
        else:
            x_ref[:, 64:80, :] = jnp.concatenate([first_late, late_rows], axis=1).astype(BF16)

    x_copy.start()
    leaves = lax.broadcasted_iota(jnp.int32, (ROWS, LEAF), 1).astype(F32) + 1.0
    weights_copy.wait()

    @pl.loop(0, LOCAL, step=UNROLL)
    def _(first):
        steps = [first + n for n in range(UNROLL)]
        logits = [
            lax.dot_general(
                x_ref[c], w_ref[c], (((1,), (1,)), ((), ())), preferred_element_type=F32
            )
            for c in steps
        ]
        residuals = []
        for c, value in zip(steps, logits):
            label = (target_ref[c] == leaves).astype(F32)
            residuals.append((jax.nn.sigmoid(value) - label).astype(BF16))
            r_ref[c] = residuals[-1]
        for c, residual in zip(steps, residuals):
            grad_ref[c] = jnp.dot(residual, w_ref[c], preferred_element_type=F32)

    r_copy.start()

    for s in range(SOURCES):
        side, i = source(s)
        rank = rank_ref[s]
        pick = (spread(rank) == places).astype(BF16).reshape(LOCAL * 8, QUERIES)
        late = jnp.where(rank >= 8.0, rank - 8.0 + 2.0 * i, -1.0)
        late_pick = (spread(late) == places).astype(BF16).reshape(LOCAL * 8, QUERIES)
        picks = jnp.concatenate([pick, late_pick], axis=0)
        near = grad_ref[:, s * 8 : s * 8 + 8, :].reshape(LOCAL * 8, WIDTH).astype(BF16)
        far = grad_ref[:, 64 + side * 8 : 72 + side * 8, :].reshape(LOCAL * 8, WIDTH).astype(BF16)
        total = lax.dot_general(
            picks,
            jnp.concatenate([near, far], axis=0),
            (((0,), (0,)), ((), ())),
            preferred_element_type=F32,
        ).astype(BF16)
        p_ref[side, i * QUERIES : (i + 1) * QUERIES, :] = total
        if i == HALF - 1:
            p_copies[side].start()
    x_copy.wait()
    r_copy.wait()
    for copy in p_copies:
        copy.wait()


def chunk(me, *stacks_and_weights):
    anywhere = pl.BlockSpec(memory_space=pl.ANY)
    return pl.pallas_call(
        chunk_kernel,
        out_shape=(
            jax.ShapeDtypeStruct((LOCAL, ROWS, WIDTH), BF16),
            jax.ShapeDtypeStruct((LOCAL, ROWS, LEAF), BF16),
            jax.ShapeDtypeStruct((CHUNK, WIDTH), BF16),
            jax.ShapeDtypeStruct((CHUNK, WIDTH), BF16),
        ),
        in_specs=[pl.BlockSpec(memory_space=pltpu.SMEM)] + [anywhere] * 5,
        out_specs=(anywhere,) * 4,
        scratch_shapes=[
            pltpu.VMEM((4, STACK, WIDTH), BF16),
            pltpu.VMEM((LOCAL, LEAF, WIDTH), BF16),
            pltpu.VMEM((LOCAL, ROWS, WIDTH), BF16),
            pltpu.VMEM((LOCAL, ROWS, LEAF), BF16),
            pltpu.VMEM((2, CHUNK, WIDTH), BF16),
            pltpu.VMEM((LOCAL, ROWS, LEAF), F32),
            pltpu.VMEM((LOCAL, ROWS, WIDTH), F32),
            pltpu.VMEM((SOURCES, LOCAL, QUERIES), F32),
            pltpu.SemaphoreType.DMA((9,)),
        ],
        compiler_params=pltpu.CompilerParams(vmem_limit_bytes=60 * MIB),
        cost_estimate=pl.CostEstimate(
            flops=8 * 10**9, bytes_accessed=20 * 10**6, transcendentals=0
        ),
    )(me, *stacks_and_weights)


def class_kernel(group_ref, *refs):
    xs, rs, outs = refs[:4], refs[4:8], refs[8:12]
    x_buf, r_buf, total_ref = refs[12:]
    group = group_ref[0]
    step = xs[0].shape[0]
    for c in range(step):
        for n in range(4):
            x_buf[n * ROWS : (n + 1) * ROWS, :] = xs[n][c]
            r_buf[n * ROWS : (n + 1) * ROWS, :] = rs[n][c]
        total_ref[...] = lax.dot_general(
            r_buf[...], x_buf[...], (((0,), (0,)), ((), ())), preferred_element_type=F32
        )
        for n in range(4):
            start = pl.multiple_of(((group + n) % 4) * 32, 32)
            outs[n][c] = total_ref[pl.ds(start, 32), :].astype(BF16)


def class_grads(group, xs, rs):
    step = 4

    def spec(rows, width):
        return pl.BlockSpec((step, rows, width), lambda c: (c, 0, 0))

    return pl.pallas_call(
        class_kernel,
        grid=(LOCAL // step,),
        out_shape=(jax.ShapeDtypeStruct((LOCAL, 32, WIDTH), BF16),) * 4,
        in_specs=[pl.BlockSpec(memory_space=pltpu.SMEM)]
        + [spec(ROWS, WIDTH)] * 4
        + [spec(ROWS, LEAF)] * 4,
        out_specs=(spec(32, WIDTH),) * 4,
        scratch_shapes=[
            pltpu.VMEM((4 * ROWS, WIDTH), BF16),
            pltpu.VMEM((4 * ROWS, LEAF), BF16),
            pltpu.VMEM((LEAF, WIDTH), F32),
        ],
        compiler_params=pltpu.CompilerParams(vmem_limit_bytes=40 * MIB),
        cost_estimate=pl.CostEstimate(
            flops=4 * 10**9, bytes_accessed=25 * 10**6, transcendentals=0
        ),
    )(group, *xs, *rs)


def body(queries, classifier, routed, positives, cluster_slot):
    weights = classifier.astype(BF16)
    me = lax.axis_index("al").astype(jnp.int32).reshape(1)
    group = lax.axis_index("pb").astype(jnp.int32).reshape(1)
    payload = payload_of(queries, routed, positives, cluster_slot)

    up, down = send(payload, NEAR_UP), send(payload, NEAR_DOWN)
    up, down, weights = lax.optimization_barrier((up, down, weights))
    cut = 144
    across_a, across_b = send(up[:cut], NEAR_UP), send(down[cut:], NEAR_DOWN)
    across = jnp.concatenate([across_a, across_b], axis=0)

    def stack(first, second):
        return jnp.concatenate(
            [first[:QUERIES], second[:QUERIES], first[QUERIES:], second[QUERIES:]], axis=0
        )

    home_a, home_b = stack(payload, up), stack(down, across)
    up_a, down_b = send(home_a, FAR_UP), send(home_b, FAR_DOWN)
    up_b, down_a = send(home_b, FAR_UP), send(home_a, FAR_DOWN)

    def run(first, second):
        return chunk(me, first, second, send(first, SWAP), send(second, SWAP), weights)

    results = [run(home_a, home_b)]
    up_a, down_b, results = lax.optimization_barrier((up_a, down_b, results))
    far_a, far_b = send(up_a, FAR_UP), send(down_b, FAR_DOWN)
    results.append(run(up_a, down_b))
    up_b, down_a, results = lax.optimization_barrier((up_b, down_a, results))
    results.append(run(down_a, up_b))
    far_a, far_b, results = lax.optimization_barrier((far_a, far_b, results))
    results.append(run(far_a, far_b))
    xs, rs = [r[0] for r in results], [r[1] for r in results]

    own, next_up, opposite, next_down = class_grads(group, xs, rs)
    cut = LOCAL // 2
    hop_up, hop_down = send_z(opposite[:cut], Z_UP), send_z(opposite[cut:], Z_DOWN)
    from_down_b = send_z(next_up[cut:], Z_UP)
    from_up_a = send_z(next_down[:cut], Z_DOWN)
    from_down_a = send_z(add(next_up[:cut], hop_up).astype(BF16), Z_UP)
    from_up_b = send_z(add(next_down[cut:], hop_down).astype(BF16), Z_DOWN)
    class_grad = jnp.concatenate(
        [add(own[:cut], from_down_a, from_up_a), add(own[cut:], from_down_b, from_up_b)], axis=0
    )

    def two_cores(result):
        total = add(result[2], send(result[3], SWAP)).astype(BF16)
        return total[: CHUNK // 2], total[CHUNK // 2 :]

    (home_a, home_b), (up_a, down_b), (down_a, up_b), (far_a, far_b) = [
        two_cores(r) for r in results
    ]

    def scatter(up_half, down_half, opposite_half, pairs_up, pairs_down):
        hop_up, hop_down = send(opposite_half[0], pairs_up), send(opposite_half[1], pairs_down)
        low_b, high_a = send(down_half[1], pairs_up), send(up_half[0], pairs_down)
        low_a = send(add(down_half[0], hop_up).astype(BF16), pairs_up)
        high_b = send(add(up_half[1], hop_down).astype(BF16), pairs_down)
        return (low_a, high_a), (low_b, high_b)

    first, second = scatter((up_a, up_b), (down_a, down_b), (far_a, far_b), FAR_UP, FAR_DOWN)
    first = add(home_a, *first)
    second = add(home_b, *second)
    mid = QUERIES // 2

    def halves(total):
        total = total.astype(BF16)
        return total[:mid], total[mid:]

    up, down, across = halves(first[QUERIES:]), halves(second[:QUERIES]), halves(second[QUERIES:])
    upper, lower = scatter(up, down, across, NEAR_UP, NEAR_DOWN)
    query_grad = jnp.concatenate(
        [add(first[:mid], *upper), add(first[mid:QUERIES], *lower)], axis=0
    )
    return query_grad, class_grad


def solution(mesh):
    return jax.shard_map(
        body,
        mesh=mesh,
        in_specs=(
            P(("pb", "al"), None),
            P("al", None, None),
            P(("pb", "al"), None),
            P(("pb", "al"), None),
            P(),
        ),
        out_specs=(P(("pb", "al"), None), P("al", "pb", None)),
        check_vma=False,
    )
```

```python
import functools

import jax
import jax.numpy as jnp
from jax import lax
from jax.experimental import pallas as pl
from jax.experimental.pallas import tpu as pltpu
from jax.sharding import PartitionSpec as P

F32 = jnp.float32
BF16 = jnp.bfloat16
SIDE = 4
QUERIES = 256
TOP = 16
WIDTH = 768
LEAF = 128
LOCAL = 32
HALF = 4
PAYLOAD = QUERIES + TOP
HEAD = 144
CHUNK = HALF * QUERIES
STACK = 2 * PAYLOAD
MIB = 1 << 20
UNROLL = 8


def al_index(x, y, core):
    return ((x % SIDE) * SIDE + y % SIDE) * 2 + core


def shift(first, second):
    pairs = []
    for x in range(SIDE):
        for y in range(SIDE):
            pairs.append((al_index(x, y, 0), al_index(x + first[0], y + first[1], 0)))
            pairs.append((al_index(x, y, 1), al_index(x + second[0], y + second[1], 1)))
    return pairs


NEAR_UP, NEAR_DOWN = shift((1, 0), (0, 1)), shift((-1, 0), (0, -1))
FAR_UP, FAR_DOWN = shift((0, 1), (1, 0)), shift((0, -1), (-1, 0))
SWAP = [(i, i ^ 1) for i in range(2 * SIDE * SIDE)]
Z_UP = [(i, (i + 1) % SIDE) for i in range(SIDE)]
Z_DOWN = [(i, (i - 1) % SIDE) for i in range(SIDE)]


def send(value, pairs):
    return lax.ppermute(value, "al", pairs)


def send_z(value, pairs):
    return lax.ppermute(value, "pb", pairs)


def add(first, *others):
    total = first.astype(F32)
    for other in others:
        total = total + other.astype(F32)
    return total


def payload_kernel(q_ref, routed_ref, positives_ref, table_ref, head_ref, tail_ref):
    head_ref[...] = q_ref[:HEAD, :]
    tail_ref[: QUERIES - HEAD, :] = q_ref[HEAD:, :]
    slots = table_ref[...]
    table = jnp.concatenate([slots // LOCAL, slots % LOCAL], axis=0).astype(F32).astype(BF16)
    lanes = lax.broadcasted_iota(jnp.int32, (128, QUERIES), 0)
    highs = lax.broadcasted_iota(jnp.int32, (8, QUERIES), 0)
    ids = routed_ref[...]
    rows = []
    for j in range(TOP):
        one = ids[j : j + 1, :]
        low = (one % 128 == lanes).astype(F32).astype(BF16)
        found = jnp.dot(table, low, preferred_element_type=F32)
        high = one // 128 == highs
        rows.append(
            jnp.concatenate(
                [
                    jnp.sum(jnp.where(high, found[:8], 0.0), axis=0, keepdims=True),
                    jnp.sum(jnp.where(high, found[8:], 0.0), axis=0, keepdims=True),
                ],
                axis=1,
            )
        )
    found = jnp.concatenate(rows, axis=0)
    labels = positives_ref[...].astype(F32)
    tail_ref[QUERIES - HEAD :, :] = jnp.concatenate([found, labels], axis=1).astype(BF16)


def payload_of(queries, routed, positives, cluster_slot):
    return pl.pallas_call(
        payload_kernel,
        out_shape=[jax.ShapeDtypeStruct((n, WIDTH), BF16) for n in (HEAD, PAYLOAD - HEAD)],
        cost_estimate=pl.CostEstimate(flops=10**8, bytes_accessed=10**6, transcendentals=0),
    )(queries, routed.T, positives.T, cluster_slot.reshape(8, 128))


def bucket_rows(groups):
    return -(-40 * groups // 16) * 16


def spread(value):
    return jnp.broadcast_to(value[:, None, :], (LOCAL, 8, QUERIES))


def late_places(rank, i):
    return jnp.where(rank >= 8.0, rank - 8.0 + 2.0 * i, -1.0)


def row_places():
    return lax.broadcasted_iota(jnp.int32, (LOCAL, 8, QUERIES), 1).astype(F32)


def select(groups, me, q_ref, copies, x_ref, target_ref, rank_ref, first_row):
    before = (
        lax.broadcasted_iota(jnp.int32, (QUERIES, QUERIES), 0)
        < lax.broadcasted_iota(jnp.int32, (QUERIES, QUERIES), 1)
    ).astype(BF16)
    clusters = lax.broadcasted_iota(jnp.int32, (LOCAL, QUERIES), 0).astype(F32)
    places = row_places()
    ones = jnp.ones((QUERIES, LEAF), BF16)
    late = []
    for group in range(groups):
        extra = []
        extra_target = []
        for i in range(HALF):
            s = group * HALF + i
            if s % 2 == 0 and s > 0:
                copies[s // 2].wait()
            start = 2 * QUERIES + s % 2 * TOP
            meta = q_ref[s // 2, start : start + TOP, :].astype(F32)
            key = jnp.where(meta[:, :QUERIES] == me, meta[:, QUERIES : 2 * QUERIES], -1.0)
            labels = meta[:, 2 * QUERIES :] + 1.0
            code = jnp.zeros((LOCAL, QUERIES), F32)
            for j in range(TOP):
                code = jnp.where(key[j : j + 1, :] == clusters, labels[j : j + 1, :], code)
            filled = code > 0.0
            rank = jnp.dot(filled.astype(BF16), before, preferred_element_type=F32)
            rank = jnp.where(filled, rank, -1.0)
            rank_ref[s] = rank
            code_rows = spread(code)

            def rows_at(place):
                match = spread(place) == places
                label = jnp.where(match, code_rows, 0.0).astype(BF16)
                return match.astype(BF16).reshape(-1, QUERIES), label.reshape(-1, QUERIES)

            pick, label = rows_at(rank)
            found = jnp.dot(
                pick,
                q_ref[s // 2, s % 2 * QUERIES : (s % 2 + 1) * QUERIES, :],
                preferred_element_type=F32,
            ).reshape(LOCAL, 8, WIDTH)
            target_ref[:, s * 8 : s * 8 + 8, :] = jnp.dot(
                label, ones, preferred_element_type=F32
            ).reshape(LOCAL, 8, LEAF)
            pick, label = rows_at(late_places(rank, i))
            extra.append(pick)
            extra_target.append(label)
            if i % 2 == 1:
                pair = jnp.concatenate([previous, found], axis=1).astype(BF16)
                row = first_row + (s - 1) * 8
                x_ref[:, row : row + 16, :] = pair
            previous = found
        late.append(
            sum(
                jnp.dot(
                    jnp.concatenate(extra[2 * n : 2 * n + 2], axis=1),
                    q_ref[2 * group + n, : 2 * QUERIES, :],
                    preferred_element_type=F32,
                )
                for n in range(2)
            ).reshape(LOCAL, 8, WIDTH)
        )
        label = sum(jnp.dot(e, ones, preferred_element_type=F32) for e in extra_target)
        row = 32 * groups + group * 8
        target_ref[:, row : row + 8, :] = label.reshape(LOCAL, 8, LEAF)
    if groups == 1:
        late.append(jnp.zeros_like(late[0]))
        target_ref[:, 40:48, :] = jnp.zeros((LOCAL, 8, LEAF), F32)
    row = first_row + 32 * groups
    x_ref[:, row : row + 16, :] = jnp.concatenate(late, axis=1).astype(BF16)


def residuals(groups, x_ref, w_ref, target_ref, r_ref, grad_ref, first_row, prepare=None):
    rows = bucket_rows(groups)
    leaves = lax.broadcasted_iota(jnp.int32, (rows, LEAF), 1).astype(F32) + 1.0

    @pl.loop(0, LOCAL, step=UNROLL)
    def _(first):
        steps = [first + n for n in range(UNROLL)]
        if prepare is not None:
            prepare(first)
        logits = [
            lax.dot_general(
                x_ref[c, first_row : first_row + rows, :],
                w_ref[c],
                (((1,), (1,)), ((), ())),
                preferred_element_type=F32,
            )
            for c in steps
        ]
        found = []
        for c, value in zip(steps, logits):
            label = (target_ref[c] == leaves).astype(F32)
            found.append((jax.nn.sigmoid(value) - label).astype(BF16))
            r_ref[c, first_row : first_row + rows, :] = found[-1]
        if grad_ref is not None:
            for c, residual in zip(steps, found):
                grad_ref[c] = jnp.dot(residual, w_ref[c], preferred_element_type=F32)


def put_back(groups, group, rank_ref, grad_ref, p_ref, p_hbm, sem):
    places = row_places()
    row = 32 * groups + group * 8
    far = grad_ref[:, row : row + 8, :].reshape(LOCAL * 8, WIDTH).astype(BF16)
    for i in range(HALF):
        s = group * HALF + i
        rank = rank_ref[s]
        picks = [
            (spread(place) == places).astype(BF16).reshape(-1, QUERIES)
            for place in (rank, late_places(rank, i))
        ]
        near = grad_ref[:, s * 8 : s * 8 + 8, :].reshape(LOCAL * 8, WIDTH).astype(BF16)
        part = pl.ds(i * QUERIES, QUERIES)
        p_ref[group, part, :] = lax.dot_general(
            jnp.concatenate(picks, axis=0),
            jnp.concatenate([near, far], axis=0),
            (((0,), (0,)), ((), ())),
            preferred_element_type=F32,
        ).astype(BF16)
        pltpu.make_async_copy(p_ref.at[group, part], p_hbm.at[part], sem).start()
    return pltpu.make_async_copy(p_ref.at[group], p_hbm, sem)


def chunk_kernel(groups, first, me_ref, *refs):
    stacks, refs = refs[: 2 * groups], refs[2 * groups :]
    w_hbm, x_hbm, r_hbm, p_hbm, refs = refs[0], refs[1], refs[2], refs[3 : 3 + groups], refs[3 + groups :]
    if first:
        rounded_hbm, wide_ref, refs = refs[0], refs[1], refs[2:]
    q_ref, w_ref, x_ref, r_ref, p_ref, target_ref, grad_ref, rank_ref, sems = refs
    copies = [
        pltpu.make_async_copy(stack, q_ref.at[n], sems.at[n]) for n, stack in enumerate(stacks)
    ]

    def weight_copy(start, count):
        part = pl.ds(start, count)
        target = wide_ref if first else w_ref
        return pltpu.make_async_copy(w_hbm.at[part], target.at[part], sems.at[9 + start // count])

    for copy in copies:
        copy.start()
    x_copy = pltpu.make_async_copy(x_ref, x_hbm, sems.at[4])
    r_copy = pltpu.make_async_copy(r_ref, r_hbm, sems.at[5])
    copies[0].wait()
    if first:
        for start in range(0, LOCAL, UNROLL):
            weight_copy(start, UNROLL).start()
    else:
        weight_copy(0, LOCAL).start()
    select(groups, me_ref[0].astype(F32), q_ref, copies, x_ref, target_ref, rank_ref, 0)
    x_copy.start()

    def round_weights(start):
        weight_copy(start, UNROLL).wait()
        for n in range(UNROLL):
            w_ref[start + n] = wide_ref[start + n].astype(BF16)

    if not first:
        weight_copy(0, LOCAL).wait()
    residuals(
        groups, x_ref, w_ref, target_ref, r_ref, grad_ref, 0, round_weights if first else None
    )
    if first:
        rounded_copy = pltpu.make_async_copy(w_ref, rounded_hbm, sems.at[8])
        rounded_copy.start()
    r_copy.start()
    p_copies = []
    for group in range(groups):
        p_copies.append(
            put_back(groups, group, rank_ref, grad_ref, p_ref, p_hbm[group], sems.at[6 + group])
        )
    if first:
        rounded_copy.wait()
    for copy in [x_copy, r_copy] + p_copies:
        copy.wait()


def scratch(groups, rows):
    return [
        pltpu.VMEM((2 * groups, STACK, WIDTH), BF16),
        pltpu.VMEM((LOCAL, LEAF, WIDTH), BF16),
        pltpu.VMEM((LOCAL, rows, WIDTH), BF16),
        pltpu.VMEM((LOCAL, rows, LEAF), BF16),
    ]


def options(flops, traffic):
    return dict(
        compiler_params=pltpu.CompilerParams(vmem_limit_bytes=60 * MIB),
        cost_estimate=pl.CostEstimate(flops=flops, bytes_accessed=traffic, transcendentals=0),
    )


ANYWHERE = pl.BlockSpec(memory_space=pl.ANY)
SCALAR = pl.BlockSpec(memory_space=pltpu.SMEM)


def chunk(me, stacks, weights):
    groups = len(stacks) // 2
    rows = bucket_rows(groups)
    first = weights.dtype == F32
    shape = (LOCAL, LEAF, WIDTH)
    return pl.pallas_call(
        functools.partial(chunk_kernel, groups, first),
        out_shape=(
            jax.ShapeDtypeStruct((LOCAL, rows, WIDTH), BF16),
            jax.ShapeDtypeStruct((LOCAL, rows, LEAF), BF16),
        )
        + (jax.ShapeDtypeStruct((CHUNK, WIDTH), BF16),) * groups
        + (jax.ShapeDtypeStruct(shape, BF16),) * first,
        in_specs=[SCALAR] + [ANYWHERE] * (len(stacks) + 1),
        out_specs=(ANYWHERE,) * (2 + groups + first),
        scratch_shapes=[pltpu.VMEM(shape, F32)] * first
        + scratch(groups, rows)
        + [
            pltpu.VMEM((groups, CHUNK, WIDTH), BF16),
            pltpu.VMEM((LOCAL, rows, LEAF), F32),
            pltpu.VMEM((LOCAL, rows, WIDTH), F32),
            pltpu.VMEM((groups * HALF, LOCAL, QUERIES), F32),
            pltpu.SemaphoreType.DMA((13,)),
        ],
        **options(4 * groups * 10**9, 10 * groups * 10**6),
    )(me, *stacks, weights)


def last_kernel(starts, me_ref, group_ref, *refs):
    stacks, w_hbm, xs, rs, refs = refs[:2], refs[2], refs[3:7], refs[7:11], refs[11:]
    (p_hbm, own, up_a, up_b, far_a, far_b, down_a, down_b), refs = refs[:8], refs[8:]
    q_ref, w_ref, x_ref, r_ref, g_ref, p_ref, target_ref, grad_ref, total_ref, rank_ref, sems = refs
    copies = [
        pltpu.make_async_copy(stack, q_ref.at[n], sems.at[n]) for n, stack in enumerate(stacks)
    ]
    weight_copy = pltpu.make_async_copy(w_hbm, w_ref, sems.at[2])
    older = []
    for n, (x, r) in enumerate(zip(xs, rs)):
        rows = pl.ds(starts[n], x.shape[1])
        older.append(pltpu.make_async_copy(x, x_ref.at[:, rows], sems.at[4 + n]))
        older.append(pltpu.make_async_copy(r, r_ref.at[:, rows], sems.at[8 + n]))
    for copy in copies:
        copy.start()
    copies[0].wait()
    for copy in [weight_copy] + older:
        copy.start()
    first_row = starts[4]
    select(1, me_ref[0].astype(F32), q_ref, copies, x_ref, target_ref, rank_ref, first_row)
    weight_copy.wait()
    residuals(1, x_ref, w_ref, target_ref, r_ref, grad_ref, first_row)
    p_copy = put_back(1, 0, rank_ref, grad_ref, p_ref, p_hbm, sems.at[12])
    for copy in older:
        copy.wait()
    group = group_ref[0]
    targets = (
        (own.at[pl.ds(0, 16)], own.at[pl.ds(16, 16)]),
        (up_a, up_b),
        (far_a, far_b),
        (down_a, down_b),
    )
    grad_copies = []
    for half in range(2):

        @pl.loop(0, 16, step=4)
        def _(first):
            for n in range(4):
                c = half * 16 + first + n
                total_ref[n] = lax.dot_general(
                    r_ref[c], x_ref[c], (((0,), (0,)), ((), ())), preferred_element_type=F32
                )
            for n in range(4):
                for away in range(4):
                    start = pl.multiple_of(((group + away) % 4) * 32, 32)
                    g_ref[2 * away + half, first + n] = total_ref[n, pl.ds(start, 32), :].astype(
                        BF16
                    )

        for away in range(4):
            place = 2 * away + half
            copy = pltpu.make_async_copy(
                g_ref.at[place], targets[away][half], sems.at[13 + place]
            )
            copy.start()
            grad_copies.append(copy)
    for copy in [p_copy] + grad_copies:
        copy.wait()


def last_chunk(me, group, stacks, weights, xs, rs):
    rows = bucket_rows(1)
    starts = [0]
    for x in xs:
        starts.append(starts[-1] + x.shape[1])
    all_rows = starts[-1] + rows
    whole = jax.ShapeDtypeStruct((LOCAL, 32, WIDTH), BF16)
    half = jax.ShapeDtypeStruct((16, 32, WIDTH), BF16)
    return pl.pallas_call(
        functools.partial(last_kernel, starts),
        out_shape=(jax.ShapeDtypeStruct((CHUNK, WIDTH), BF16),) + (whole,) + (half,) * 6,
        in_specs=[SCALAR] * 2 + [ANYWHERE] * 11,
        out_specs=(ANYWHERE,) * 8,
        scratch_shapes=scratch(1, all_rows)
        + [
            pltpu.VMEM((8, 16, 32, WIDTH), BF16),
            pltpu.VMEM((1, CHUNK, WIDTH), BF16),
            pltpu.VMEM((LOCAL, rows, LEAF), F32),
            pltpu.VMEM((LOCAL, rows, WIDTH), F32),
            pltpu.VMEM((4, LEAF, WIDTH), F32),
            pltpu.VMEM((HALF, LOCAL, QUERIES), F32),
            pltpu.SemaphoreType.DMA((21,)),
        ],
        **options(8 * 10**9, 40 * 10**6),
    )(me, group, *stacks, weights, *xs, *rs)


def class_sum_kernel(own_ref, low_refs, high_refs, out_hbm, out_ref, sems):
    copies = []
    for n in range(4):
        part = slice(8 * n, 8 * n + 8)
        half = slice(8 * (n % 2), 8 * (n % 2) + 8)
        out_ref[part] = add(own_ref[part], *[ref[half] for ref in (low_refs, high_refs)[n // 2]])
        copies.append(pltpu.make_async_copy(out_ref.at[part], out_hbm.at[part], sems.at[n]))
        copies[-1].start()
    for copy in copies:
        copy.wait()


def class_sum(own, low, high):
    in_vmem = pl.BlockSpec(memory_space=pltpu.VMEM)
    return pl.pallas_call(
        class_sum_kernel,
        out_shape=jax.ShapeDtypeStruct((LOCAL, 32, WIDTH), F32),
        in_specs=[in_vmem, (in_vmem,) * 2, (in_vmem,) * 2],
        out_specs=ANYWHERE,
        scratch_shapes=[pltpu.VMEM((LOCAL, 32, WIDTH), F32), pltpu.SemaphoreType.DMA((4,))],
        compiler_params=pltpu.CompilerParams(vmem_limit_bytes=24 * MIB),
        cost_estimate=pl.CostEstimate(flops=10**6, bytes_accessed=8 * 10**6, transcendentals=0),
    )(own, low, high)


def body(queries, classifier, routed, positives, cluster_slot):
    me = lax.axis_index("al").astype(jnp.int32).reshape(1)
    group = lax.axis_index("pb").astype(jnp.int32).reshape(1)
    payload = payload_of(queries, routed, positives, cluster_slot)

    up = [send(piece, NEAR_UP) for piece in payload]
    down = [send(piece, NEAR_DOWN) for piece in payload]
    across = [send(up[0], NEAR_UP), send(down[1], NEAR_DOWN)]

    def stack(first, second):
        cut = QUERIES - HEAD
        return jnp.concatenate(
            [first[0], first[1][:cut], second[0], second[1][:cut], first[1][cut:], second[1][cut:]],
            axis=0,
        )

    def swap(stacks):
        return [send(s, SWAP) for s in stacks]

    home = [stack(payload, up), stack(down, across)]
    home = lax.optimization_barrier(home)
    near_half = [send(home[0], FAR_UP), send(home[1], FAR_DOWN)]
    x, r, p_home, weights = chunk(me, home, classifier)
    xs, rs = [x], [r]
    near_half, home, xs = lax.optimization_barrier((near_half, home, xs))
    far_half = [send(home[0], FAR_DOWN), send(home[1], FAR_UP)]
    x, r, p_near, q_home = chunk(me, near_half + swap(home), weights)
    far_half, near_half, x, r = lax.optimization_barrier((far_half, near_half, x, r))
    xs.append(x), rs.append(r)
    last = [send(near_half[0], FAR_UP), send(near_half[1], FAR_DOWN)]
    x, r, p_far, q_near = chunk(me, far_half + swap(near_half), weights)
    last, x, r = lax.optimization_barrier((last, x, r))
    xs.append(x), rs.append(r)

    def two_cores(mine, other):
        total = add(mine, send(other, SWAP)).astype(BF16)
        return total[: CHUNK // 2], total[CHUNK // 2 :]

    x, r, p_last, q_far = chunk(me, last + swap(far_half), weights)
    xs.append(x), rs.append(r)
    outs = last_chunk(me, group, swap(last), weights, xs, rs)
    q_last, own, next_up_a, next_up_b, opposite_a, opposite_b, next_down_a, next_down_b = outs

    far_a, far_b = two_cores(p_last, q_last)
    arrived = lax.optimization_barrier(
        (
            send_z(opposite_a, Z_UP),
            send_z(opposite_b, Z_DOWN),
            send(far_a, FAR_UP),
            send(far_b, FAR_DOWN),
        )
    )
    class_below, class_above, from_low, from_high = arrived

    up_a, down_b = two_cores(p_near, q_near)
    down_a, up_b = two_cores(p_far, q_far)
    sends = (
        add(next_up_a, class_below).astype(BF16),
        add(next_down_b, class_above).astype(BF16),
        jnp.concatenate([add(down_a, from_low).astype(BF16), down_b]),
        jnp.concatenate([up_a, add(up_b, from_high).astype(BF16)]),
        next_up_b,
        next_down_a,
    )
    class_to_up, class_to_down, to_up, to_down, *rest = lax.optimization_barrier(sends)
    arrived = lax.optimization_barrier(
        (
            send_z(class_to_up, Z_UP),
            send_z(class_to_down, Z_DOWN),
            send(to_up, FAR_UP),
            send(to_down, FAR_DOWN),
            *rest,
        )
    )
    sum_below_a, sum_above_b, from_low, from_high, next_up_b, next_down_a = arrived

    home_a, home_b = two_cores(p_home, q_home)
    cut = CHUNK // 2
    first = add(home_a, from_low[:cut], from_high[:cut])
    second = add(home_b, from_low[cut:], from_high[cut:])
    mid = QUERIES // 2

    def halves(total):
        total = total.astype(BF16)
        return total[:mid], total[mid:]

    below_b, above_a = send_z(next_up_b, Z_UP), send_z(next_down_a, Z_DOWN)
    up, down, across = halves(first[QUERIES:]), halves(second[:QUERIES]), halves(second[QUERIES:])
    low = send(jnp.concatenate([across[0], down[1]]), NEAR_UP)
    high = send(jnp.concatenate([up[0], across[1]]), NEAR_DOWN)
    low_sum = send(add(down[0], low[:mid]).astype(BF16), NEAR_UP)
    high_sum = send(add(up[1], high[mid:]).astype(BF16), NEAR_DOWN)
    query_grad = jnp.concatenate(
        [add(first[:mid], low_sum, high[:mid]), add(first[mid:QUERIES], low[mid:], high_sum)],
        axis=0,
    )
    below_b, above_a, query_grad = lax.optimization_barrier((below_b, above_a, query_grad))
    class_grad = class_sum(own, (sum_below_a, above_a), (below_b, sum_above_b))
    return query_grad, class_grad


def solution(mesh):
    return jax.shard_map(
        body,
        mesh=mesh,
        in_specs=(
            P(("pb", "al"), None),
            P("al", None, None),
            P(("pb", "al"), None),
            P(("pb", "al"), None),
            P(),
        ),
        out_specs=(P(("pb", "al"), None), P("al", "pb", None)),
        check_vma=False,
    )
```

```python
import functools

import jax
import jax.numpy as jnp
from jax import lax
from jax.experimental import pallas as pl
from jax.experimental.pallas import tpu as pltpu
from jax.sharding import PartitionSpec as P

F32 = jnp.float32
BF16 = jnp.bfloat16
SIDE = 4
QUERIES = 256
TOP = 16
WIDTH = 768
LEAF = 128
LOCAL = 32
HALF = 4
PAYLOAD = QUERIES + TOP
CHUNK = HALF * QUERIES
STACK = 2 * PAYLOAD
MIB = 1 << 20
UNROLL = 8


def al_index(x, y, core):
    return ((x % SIDE) * SIDE + y % SIDE) * 2 + core


def shift(first, second):
    pairs = []
    for x in range(SIDE):
        for y in range(SIDE):
            pairs.append((al_index(x, y, 0), al_index(x + first[0], y + first[1], 0)))
            pairs.append((al_index(x, y, 1), al_index(x + second[0], y + second[1], 1)))
    return pairs


NEAR_UP, NEAR_DOWN = shift((1, 0), (0, 1)), shift((-1, 0), (0, -1))
FAR_UP, FAR_DOWN = shift((0, 1), (1, 0)), shift((0, -1), (-1, 0))
SWAP = [(i, i ^ 1) for i in range(2 * SIDE * SIDE)]
Z_UP = [(i, (i + 1) % SIDE) for i in range(SIDE)]
Z_DOWN = [(i, (i - 1) % SIDE) for i in range(SIDE)]


def send(value, pairs):
    return lax.ppermute(value, "al", pairs)


def send_z(value, pairs):
    return lax.ppermute(value, "pb", pairs)


def add(first, *others):
    total = first.astype(F32)
    for other in others:
        total = total + other.astype(F32)
    return total


def payload_kernel(q_ref, routed_ref, positives_ref, table_ref, out_ref):
    out_ref[:QUERIES, :] = q_ref[...]
    slots = table_ref[...]
    table = jnp.concatenate([slots // LOCAL, slots % LOCAL], axis=0).astype(F32).astype(BF16)
    lanes = lax.broadcasted_iota(jnp.int32, (128, QUERIES), 0)
    highs = lax.broadcasted_iota(jnp.int32, (8, QUERIES), 0)
    ids = routed_ref[...]
    rows = []
    for j in range(TOP):
        one = ids[j : j + 1, :]
        low = (one % 128 == lanes).astype(F32).astype(BF16)
        found = jnp.dot(table, low, preferred_element_type=F32)
        high = one // 128 == highs
        rows.append(
            jnp.concatenate(
                [
                    jnp.sum(jnp.where(high, found[:8], 0.0), axis=0, keepdims=True),
                    jnp.sum(jnp.where(high, found[8:], 0.0), axis=0, keepdims=True),
                ],
                axis=1,
            )
        )
    found = jnp.concatenate(rows, axis=0)
    labels = positives_ref[...].astype(F32)
    out_ref[QUERIES:, :] = jnp.concatenate([found, labels], axis=1).astype(BF16)


def payload_of(queries, routed, positives, cluster_slot):
    return pl.pallas_call(
        payload_kernel,
        out_shape=jax.ShapeDtypeStruct((PAYLOAD, WIDTH), BF16),
        cost_estimate=pl.CostEstimate(flops=10**8, bytes_accessed=10**6, transcendentals=0),
    )(queries, routed.T, positives.T, cluster_slot.reshape(8, 128))


def bucket_rows(groups):
    return -(-40 * groups // 16) * 16


def spread(value):
    return jnp.broadcast_to(value[:, None, :], (LOCAL, 8, QUERIES))


def late_places(rank, i):
    return jnp.where(rank >= 8.0, rank - 8.0 + 2.0 * i, -1.0)


def row_places():
    return lax.broadcasted_iota(jnp.int32, (LOCAL, 8, QUERIES), 1).astype(F32)


def select(groups, me, q_ref, copies, x_ref, target_ref, rank_ref, first_row):
    before = (
        lax.broadcasted_iota(jnp.int32, (QUERIES, QUERIES), 0)
        < lax.broadcasted_iota(jnp.int32, (QUERIES, QUERIES), 1)
    ).astype(BF16)
    clusters = lax.broadcasted_iota(jnp.int32, (LOCAL, QUERIES), 0).astype(F32)
    places = row_places()
    ones = jnp.ones((QUERIES, LEAF), BF16)
    late = []
    for group in range(groups):
        extra = []
        extra_target = []
        for i in range(HALF):
            s = group * HALF + i
            if s % 2 == 0 and s > 0:
                copies[s // 2].wait()
            start = 2 * QUERIES + s % 2 * TOP
            meta = q_ref[s // 2, start : start + TOP, :].astype(F32)
            key = jnp.where(meta[:, :QUERIES] == me, meta[:, QUERIES : 2 * QUERIES], -1.0)
            labels = meta[:, 2 * QUERIES :] + 1.0
            code = jnp.zeros((LOCAL, QUERIES), F32)
            for j in range(TOP):
                code = jnp.where(key[j : j + 1, :] == clusters, labels[j : j + 1, :], code)
            filled = code > 0.0
            rank = jnp.dot(filled.astype(BF16), before, preferred_element_type=F32)
            rank = jnp.where(filled, rank, -1.0)
            rank_ref[s] = rank
            code_rows = spread(code)

            def rows_at(place):
                match = spread(place) == places
                label = jnp.where(match, code_rows, 0.0).astype(BF16)
                return match.astype(BF16).reshape(-1, QUERIES), label.reshape(-1, QUERIES)

            pick, label = rows_at(rank)
            found = jnp.dot(
                pick,
                q_ref[s // 2, s % 2 * QUERIES : (s % 2 + 1) * QUERIES, :],
                preferred_element_type=F32,
            ).reshape(LOCAL, 8, WIDTH)
            target_ref[:, s * 8 : s * 8 + 8, :] = jnp.dot(
                label, ones, preferred_element_type=F32
            ).reshape(LOCAL, 8, LEAF)
            pick, label = rows_at(late_places(rank, i))
            extra.append(pick)
            extra_target.append(label)
            if i % 2 == 1:
                pair = jnp.concatenate([previous, found], axis=1).astype(BF16)
                row = first_row + (s - 1) * 8
                x_ref[:, row : row + 16, :] = pair
            previous = found
        late.append(
            sum(
                jnp.dot(
                    jnp.concatenate(extra[2 * n : 2 * n + 2], axis=1),
                    q_ref[2 * group + n, : 2 * QUERIES, :],
                    preferred_element_type=F32,
                )
                for n in range(2)
            ).reshape(LOCAL, 8, WIDTH)
        )
        label = sum(jnp.dot(e, ones, preferred_element_type=F32) for e in extra_target)
        row = 32 * groups + group * 8
        target_ref[:, row : row + 8, :] = label.reshape(LOCAL, 8, LEAF)
    if groups == 1:
        late.append(jnp.zeros_like(late[0]))
        target_ref[:, 40:48, :] = jnp.zeros((LOCAL, 8, LEAF), F32)
    row = first_row + 32 * groups
    x_ref[:, row : row + 16, :] = jnp.concatenate(late, axis=1).astype(BF16)


def residuals(groups, x_ref, w_ref, target_ref, r_ref, grad_ref, first_row, prepare=None):
    rows = bucket_rows(groups)
    leaves = lax.broadcasted_iota(jnp.int32, (rows, LEAF), 1).astype(F32) + 1.0

    @pl.loop(0, LOCAL, step=UNROLL)
    def _(first):
        steps = [first + n for n in range(UNROLL)]
        if prepare is not None:
            prepare(first)
        logits = [
            lax.dot_general(
                x_ref[c, first_row : first_row + rows, :],
                w_ref[c],
                (((1,), (1,)), ((), ())),
                preferred_element_type=F32,
            )
            for c in steps
        ]
        found = []
        for c, value in zip(steps, logits):
            label = (target_ref[c] == leaves).astype(F32)
            found.append((jax.nn.sigmoid(value) - label).astype(BF16))
            r_ref[c, first_row : first_row + rows, :] = found[-1]
        if grad_ref is not None:
            for c, residual in zip(steps, found):
                grad_ref[c] = jnp.dot(residual, w_ref[c], preferred_element_type=F32)


def put_back(groups, group, rank_ref, grad_ref, p_ref, p_hbm, sem):
    places = row_places()
    row = 32 * groups + group * 8
    far = grad_ref[:, row : row + 8, :].reshape(LOCAL * 8, WIDTH).astype(BF16)
    for i in range(HALF):
        s = group * HALF + i
        rank = rank_ref[s]
        picks = [
            (spread(place) == places).astype(BF16).reshape(-1, QUERIES)
            for place in (rank, late_places(rank, i))
        ]
        near = grad_ref[:, s * 8 : s * 8 + 8, :].reshape(LOCAL * 8, WIDTH).astype(BF16)
        part = pl.ds(i * QUERIES, QUERIES)
        p_ref[group, part, :] = lax.dot_general(
            jnp.concatenate(picks, axis=0),
            jnp.concatenate([near, far], axis=0),
            (((0,), (0,)), ((), ())),
            preferred_element_type=F32,
        ).astype(BF16)
        pltpu.make_async_copy(p_ref.at[group, part], p_hbm.at[part], sem).start()
    return pltpu.make_async_copy(p_ref.at[group], p_hbm, sem)


def chunk_kernel(groups, first, me_ref, *refs):
    stacks, refs = refs[: 2 * groups], refs[2 * groups :]
    w_hbm, x_hbm, r_hbm, p_hbm, refs = refs[0], refs[1], refs[2], refs[3 : 3 + groups], refs[3 + groups :]
    if first:
        rounded_hbm, wide_ref, refs = refs[0], refs[1], refs[2:]
    q_ref, w_ref, x_ref, r_ref, p_ref, target_ref, grad_ref, rank_ref, sems = refs
    copies = [
        pltpu.make_async_copy(stack, q_ref.at[n], sems.at[n]) for n, stack in enumerate(stacks)
    ]

    def weight_copy(start, count):
        part = pl.ds(start, count)
        target = wide_ref if first else w_ref
        return pltpu.make_async_copy(w_hbm.at[part], target.at[part], sems.at[9 + start // count])

    for copy in copies:
        copy.start()
    x_copy = pltpu.make_async_copy(x_ref, x_hbm, sems.at[4])
    r_copy = pltpu.make_async_copy(r_ref, r_hbm, sems.at[5])
    copies[0].wait()
    if first:
        for start in range(0, LOCAL, UNROLL):
            weight_copy(start, UNROLL).start()
    else:
        weight_copy(0, LOCAL).start()
    select(groups, me_ref[0].astype(F32), q_ref, copies, x_ref, target_ref, rank_ref, 0)
    x_copy.start()

    def round_weights(start):
        weight_copy(start, UNROLL).wait()
        for n in range(UNROLL):
            w_ref[start + n] = wide_ref[start + n].astype(BF16)

    if not first:
        weight_copy(0, LOCAL).wait()
    residuals(
        groups, x_ref, w_ref, target_ref, r_ref, grad_ref, 0, round_weights if first else None
    )
    if first:
        rounded_copy = pltpu.make_async_copy(w_ref, rounded_hbm, sems.at[8])
        rounded_copy.start()
    r_copy.start()
    p_copies = []
    for group in range(groups):
        p_copies.append(
            put_back(groups, group, rank_ref, grad_ref, p_ref, p_hbm[group], sems.at[6 + group])
        )
    if first:
        rounded_copy.wait()
    for copy in [x_copy, r_copy] + p_copies:
        copy.wait()


def scratch(groups, rows):
    return [
        pltpu.VMEM((2 * groups, STACK, WIDTH), BF16),
        pltpu.VMEM((LOCAL, LEAF, WIDTH), BF16),
        pltpu.VMEM((LOCAL, rows, WIDTH), BF16),
        pltpu.VMEM((LOCAL, rows, LEAF), BF16),
    ]


def options(flops, traffic):
    return dict(
        compiler_params=pltpu.CompilerParams(vmem_limit_bytes=60 * MIB),
        cost_estimate=pl.CostEstimate(flops=flops, bytes_accessed=traffic, transcendentals=0),
    )


ANYWHERE = pl.BlockSpec(memory_space=pl.ANY)
SCALAR = pl.BlockSpec(memory_space=pltpu.SMEM)


def chunk(me, stacks, weights):
    groups = len(stacks) // 2
    rows = bucket_rows(groups)
    first = weights.dtype == F32
    shape = (LOCAL, LEAF, WIDTH)
    return pl.pallas_call(
        functools.partial(chunk_kernel, groups, first),
        out_shape=(
            jax.ShapeDtypeStruct((LOCAL, rows, WIDTH), BF16),
            jax.ShapeDtypeStruct((LOCAL, rows, LEAF), BF16),
        )
        + (jax.ShapeDtypeStruct((CHUNK, WIDTH), BF16),) * groups
        + (jax.ShapeDtypeStruct(shape, BF16),) * first,
        in_specs=[SCALAR] + [ANYWHERE] * (len(stacks) + 1),
        out_specs=(ANYWHERE,) * (2 + groups + first),
        scratch_shapes=[pltpu.VMEM(shape, F32)] * first
        + scratch(groups, rows)
        + [
            pltpu.VMEM((groups, CHUNK, WIDTH), BF16),
            pltpu.VMEM((LOCAL, rows, LEAF), F32),
            pltpu.VMEM((LOCAL, rows, WIDTH), F32),
            pltpu.VMEM((groups * HALF, LOCAL, QUERIES), F32),
            pltpu.SemaphoreType.DMA((13,)),
        ],
        **options(4 * groups * 10**9, 10 * groups * 10**6),
    )(me, *stacks, weights)


def last_kernel(starts, me_ref, group_ref, *refs):
    stacks, w_hbm, xs, rs, refs = refs[:2], refs[2], refs[3:7], refs[7:11], refs[11:]
    (p_hbm, own, up_a, up_b, far_a, far_b, down_a, down_b), refs = refs[:8], refs[8:]
    q_ref, w_ref, x_ref, r_ref, g_ref, p_ref, target_ref, grad_ref, total_ref, rank_ref, sems = refs
    copies = [
        pltpu.make_async_copy(stack, q_ref.at[n], sems.at[n]) for n, stack in enumerate(stacks)
    ]
    weight_copy = pltpu.make_async_copy(w_hbm, w_ref, sems.at[2])
    older = []
    for quarter in range(4):
        part = pl.ds(8 * quarter, 8)
        for n in range(4):
            rows = pl.ds(starts[n], xs[n].shape[1])
            place = 22 + 8 * quarter + 2 * n
            older.append(
                pltpu.make_async_copy(xs[n].at[part], x_ref.at[part, rows], sems.at[place])
            )
            older.append(
                pltpu.make_async_copy(rs[n].at[part], r_ref.at[part, rows], sems.at[place + 1])
            )
    for copy in copies + [weight_copy] + older[:16]:
        copy.start()
    copies[0].wait()
    first_row = starts[4]
    select(1, me_ref[0].astype(F32), q_ref, copies, x_ref, target_ref, rank_ref, first_row)
    for copy in older[16:]:
        copy.start()
    weight_copy.wait()
    residuals(1, x_ref, w_ref, target_ref, r_ref, grad_ref, first_row)
    p_copy = put_back(1, 0, rank_ref, grad_ref, p_ref, p_hbm, sems.at[12])
    group = group_ref[0]
    targets = (
        (own.at[pl.ds(0, 16)], own.at[pl.ds(16, 16)]),
        (up_a, up_b),
        (far_a, far_b),
        (down_a, down_b),
    )
    grad_copies = []
    for quarter in range(4):
        for copy in older[8 * quarter : 8 * quarter + 8]:
            copy.wait()

        @pl.loop(0, 8, step=4)
        def _(first):
            for n in range(4):
                c = quarter * 8 + first + n
                total_ref[n] = lax.dot_general(
                    r_ref[c], x_ref[c], (((0,), (0,)), ((), ())), preferred_element_type=F32
                )
            for n in range(4):
                for away in range(4):
                    start = pl.multiple_of(((group + away) % 4) * 32, 32)
                    place = 2 * away + quarter // 2
                    g_ref[place, quarter % 2 * 8 + first + n] = total_ref[
                        n, pl.ds(start, 32), :
                    ].astype(BF16)

        for away in range(4):
            part = pl.ds(quarter % 2 * 8, 8)
            copy = pltpu.make_async_copy(
                g_ref.at[2 * away + quarter // 2, part],
                targets[away][quarter // 2].at[part],
                sems.at[54 + 4 * quarter + away],
            )
            copy.start()
            grad_copies.append(copy)
    for copy in [p_copy] + grad_copies:
        copy.wait()


def last_chunk(me, group, stacks, weights, xs, rs):
    rows = bucket_rows(1)
    starts = [0]
    for x in xs:
        starts.append(starts[-1] + x.shape[1])
    all_rows = starts[-1] + rows
    whole = jax.ShapeDtypeStruct((LOCAL, 32, WIDTH), BF16)
    half = jax.ShapeDtypeStruct((16, 32, WIDTH), BF16)
    return pl.pallas_call(
        functools.partial(last_kernel, starts),
        out_shape=(jax.ShapeDtypeStruct((CHUNK, WIDTH), BF16),) + (whole,) + (half,) * 6,
        in_specs=[SCALAR] * 2 + [ANYWHERE] * 11,
        out_specs=(ANYWHERE,) * 8,
        scratch_shapes=scratch(1, all_rows)
        + [
            pltpu.VMEM((8, 16, 32, WIDTH), BF16),
            pltpu.VMEM((1, CHUNK, WIDTH), BF16),
            pltpu.VMEM((LOCAL, rows, LEAF), F32),
            pltpu.VMEM((LOCAL, rows, WIDTH), F32),
            pltpu.VMEM((4, LEAF, WIDTH), F32),
            pltpu.VMEM((HALF, LOCAL, QUERIES), F32),
            pltpu.SemaphoreType.DMA((70,)),
        ],
        **options(8 * 10**9, 40 * 10**6),
    )(me, group, *stacks, weights, *xs, *rs)


def class_sum_kernel(own_ref, low_refs, high_refs, out_hbm, out_ref, sems):
    copies = []
    for n in range(4):
        part = slice(8 * n, 8 * n + 8)
        half = slice(8 * (n % 2), 8 * (n % 2) + 8)
        out_ref[part] = add(own_ref[part], *[ref[half] for ref in (low_refs, high_refs)[n // 2]])
        copies.append(pltpu.make_async_copy(out_ref.at[part], out_hbm.at[part], sems.at[n]))
        copies[-1].start()
    for copy in copies:
        copy.wait()


def class_sum(own, low, high):
    in_vmem = pl.BlockSpec(memory_space=pltpu.VMEM)
    return pl.pallas_call(
        class_sum_kernel,
        out_shape=jax.ShapeDtypeStruct((LOCAL, 32, WIDTH), F32),
        in_specs=[in_vmem, (in_vmem,) * 2, (in_vmem,) * 2],
        out_specs=ANYWHERE,
        scratch_shapes=[pltpu.VMEM((LOCAL, 32, WIDTH), F32), pltpu.SemaphoreType.DMA((4,))],
        compiler_params=pltpu.CompilerParams(vmem_limit_bytes=24 * MIB),
        cost_estimate=pl.CostEstimate(flops=10**6, bytes_accessed=8 * 10**6, transcendentals=0),
    )(own, low, high)


def body(queries, classifier, routed, positives, cluster_slot):
    me = lax.axis_index("al").astype(jnp.int32).reshape(1)
    group = lax.axis_index("pb").astype(jnp.int32).reshape(1)
    payload = payload_of(queries, routed, positives, cluster_slot)

    up, down = send(payload, NEAR_UP), send(payload, NEAR_DOWN)
    cut = 144
    across = jnp.concatenate([send(up[:cut], NEAR_UP), send(down[cut:], NEAR_DOWN)], axis=0)

    def stack(first, second):
        return jnp.concatenate(
            [first[:QUERIES], second[:QUERIES], first[QUERIES:], second[QUERIES:]], axis=0
        )

    def swap(stacks):
        return [send(s, SWAP) for s in stacks]

    home = [stack(payload, up), stack(down, across)]
    home = lax.optimization_barrier(home)
    near_half = [send(home[0], FAR_UP), send(home[1], FAR_DOWN)]
    x, r, p_home, weights = chunk(me, home, classifier)
    xs, rs = [x], [r]
    near_half, home, xs = lax.optimization_barrier((near_half, home, xs))
    far_half = [send(home[0], FAR_DOWN), send(home[1], FAR_UP)]
    x, r, p_near, q_home = chunk(me, near_half + swap(home), weights)
    far_half, near_half, x, r = lax.optimization_barrier((far_half, near_half, x, r))
    xs.append(x), rs.append(r)
    last = [send(near_half[0], FAR_UP), send(near_half[1], FAR_DOWN)]
    x, r, p_far, q_near = chunk(me, far_half + swap(near_half), weights)
    last, x, r = lax.optimization_barrier((last, x, r))
    xs.append(x), rs.append(r)

    def two_cores(mine, other):
        total = add(mine, send(other, SWAP)).astype(BF16)
        return total[: CHUNK // 2], total[CHUNK // 2 :]

    x, r, p_last, q_far = chunk(me, last + swap(far_half), weights)
    xs.append(x), rs.append(r)
    outs = last_chunk(me, group, swap(last), weights, xs, rs)
    q_last, own, next_up_a, next_up_b, opposite_a, opposite_b, next_down_a, next_down_b = outs

    far_a, far_b = two_cores(p_last, q_last)
    arrived = lax.optimization_barrier(
        (
            send_z(opposite_a, Z_UP),
            send_z(opposite_b, Z_DOWN),
            send(far_a, FAR_UP),
            send(far_b, FAR_DOWN),
        )
    )
    class_below, class_above, from_low, from_high = arrived

    up_a, down_b = two_cores(p_near, q_near)
    down_a, up_b = two_cores(p_far, q_far)
    sends = (
        add(next_up_a, class_below).astype(BF16),
        add(next_down_b, class_above).astype(BF16),
        jnp.concatenate([add(down_a, from_low).astype(BF16), down_b]),
        jnp.concatenate([up_a, add(up_b, from_high).astype(BF16)]),
        next_up_b,
        next_down_a,
    )
    class_to_up, class_to_down, to_up, to_down, *rest = lax.optimization_barrier(sends)
    arrived = lax.optimization_barrier(
        (
            send_z(class_to_up, Z_UP),
            send_z(class_to_down, Z_DOWN),
            send(to_up, FAR_UP),
            send(to_down, FAR_DOWN),
            *rest,
        )
    )
    sum_below_a, sum_above_b, from_low, from_high, next_up_b, next_down_a = arrived

    home_a, home_b = two_cores(p_home, q_home)
    cut = CHUNK // 2
    first = add(home_a, from_low[:cut], from_high[:cut])
    second = add(home_b, from_low[cut:], from_high[cut:])
    mid = QUERIES // 2

    def halves(total):
        total = total.astype(BF16)
        return total[:mid], total[mid:]

    below_b, above_a = send_z(next_up_b, Z_UP), send_z(next_down_a, Z_DOWN)
    up, down, across = halves(first[QUERIES:]), halves(second[:QUERIES]), halves(second[QUERIES:])
    low = send(jnp.concatenate([across[0], down[1]]), NEAR_UP)
    high = send(jnp.concatenate([up[0], across[1]]), NEAR_DOWN)
    low_sum = send(add(down[0], low[:mid]).astype(BF16), NEAR_UP)
    high_sum = send(add(up[1], high[mid:]).astype(BF16), NEAR_DOWN)
    query_grad = jnp.concatenate(
        [add(first[:mid], low_sum, high[:mid]), add(first[mid:QUERIES], low[mid:], high_sum)],
        axis=0,
    )
    below_b, above_a, query_grad = lax.optimization_barrier((below_b, above_a, query_grad))
    class_grad = class_sum(own, (sum_below_a, above_a), (below_b, sum_above_b))
    return query_grad, class_grad


def solution(mesh):
    return jax.shard_map(
        body,
        mesh=mesh,
        in_specs=(
            P(("pb", "al"), None),
            P("al", None, None),
            P(("pb", "al"), None),
            P(("pb", "al"), None),
            P(),
        ),
        out_specs=(P(("pb", "al"), None), P("al", "pb", None)),
        check_vma=False,
    )
```

```python
import functools

import jax
import jax.numpy as jnp
from jax import lax
from jax.experimental import pallas as pl
from jax.experimental.pallas import tpu as pltpu
from jax.sharding import PartitionSpec as P

F32 = jnp.float32
BF16 = jnp.bfloat16
SIDE = 4
QUERIES = 256
TOP = 16
WIDTH = 768
LEAF = 128
LOCAL = 32
HALF = 4
PAYLOAD = QUERIES + TOP
CHUNK = HALF * QUERIES
STACK = 2 * PAYLOAD
MIB = 1 << 20
UNROLL = 8


def al_index(x, y, core):
    return ((x % SIDE) * SIDE + y % SIDE) * 2 + core


def shift(first, second):
    pairs = []
    for x in range(SIDE):
        for y in range(SIDE):
            pairs.append((al_index(x, y, 0), al_index(x + first[0], y + first[1], 0)))
            pairs.append((al_index(x, y, 1), al_index(x + second[0], y + second[1], 1)))
    return pairs


NEAR_UP, NEAR_DOWN = shift((1, 0), (0, 1)), shift((-1, 0), (0, -1))
FAR_UP, FAR_DOWN = shift((0, 1), (1, 0)), shift((0, -1), (-1, 0))
SWAP = [(i, i ^ 1) for i in range(2 * SIDE * SIDE)]
Z_UP = [(i, (i + 1) % SIDE) for i in range(SIDE)]
Z_DOWN = [(i, (i - 1) % SIDE) for i in range(SIDE)]


def send(value, pairs):
    return lax.ppermute(value, "al", pairs)


def send_z(value, pairs):
    return lax.ppermute(value, "pb", pairs)


def add(first, *others):
    total = first.astype(F32)
    for other in others:
        total = total + other.astype(F32)
    return total


def payload_kernel(q_ref, routed_ref, positives_ref, table_ref, out_ref):
    out_ref[:QUERIES, :] = q_ref[...]
    slots = table_ref[...]
    table = jnp.concatenate([slots // LOCAL, slots % LOCAL], axis=0).astype(F32).astype(BF16)
    lanes = lax.broadcasted_iota(jnp.int32, (128, QUERIES), 0)
    highs = lax.broadcasted_iota(jnp.int32, (8, QUERIES), 0)
    ids = routed_ref[...]
    rows = []
    for j in range(TOP):
        one = ids[j : j + 1, :]
        low = (one % 128 == lanes).astype(F32).astype(BF16)
        found = jnp.dot(table, low, preferred_element_type=F32)
        high = one // 128 == highs
        rows.append(
            jnp.concatenate(
                [
                    jnp.sum(jnp.where(high, found[:8], 0.0), axis=0, keepdims=True),
                    jnp.sum(jnp.where(high, found[8:], 0.0), axis=0, keepdims=True),
                ],
                axis=1,
            )
        )
    found = jnp.concatenate(rows, axis=0)
    labels = positives_ref[...].astype(F32)
    out_ref[QUERIES:, :] = jnp.concatenate([found, labels], axis=1).astype(BF16)


def payload_of(queries, routed, positives, cluster_slot):
    return pl.pallas_call(
        payload_kernel,
        out_shape=jax.ShapeDtypeStruct((PAYLOAD, WIDTH), BF16),
        cost_estimate=pl.CostEstimate(flops=10**8, bytes_accessed=10**6, transcendentals=0),
    )(queries, routed.T, positives.T, cluster_slot.reshape(8, 128))


def bucket_rows(groups):
    return -(-40 * groups // 16) * 16


def spread(value):
    return jnp.broadcast_to(value[:, None, :], (LOCAL, 8, QUERIES))


def late_places(rank, i):
    return jnp.where(rank >= 8.0, rank - 8.0 + 2.0 * i, -1.0)


def row_places():
    return lax.broadcasted_iota(jnp.int32, (LOCAL, 8, QUERIES), 1).astype(F32)


def select(groups, me, q_ref, copies, x_ref, target_ref, rank_ref, first_row):
    before = (
        lax.broadcasted_iota(jnp.int32, (QUERIES, QUERIES), 0)
        < lax.broadcasted_iota(jnp.int32, (QUERIES, QUERIES), 1)
    ).astype(BF16)
    clusters = lax.broadcasted_iota(jnp.int32, (LOCAL, QUERIES), 0).astype(F32)
    places = row_places()
    ones = jnp.ones((QUERIES, LEAF), BF16)
    late = []
    for group in range(groups):
        extra = []
        extra_target = []
        for i in range(HALF):
            s = group * HALF + i
            if s % 2 == 0 and s > 0:
                copies[s // 2].wait()
            start = 2 * QUERIES + s % 2 * TOP
            meta = q_ref[s // 2, start : start + TOP, :].astype(F32)
            key = jnp.where(meta[:, :QUERIES] == me, meta[:, QUERIES : 2 * QUERIES], -1.0)
            labels = meta[:, 2 * QUERIES :] + 1.0
            code = jnp.zeros((LOCAL, QUERIES), F32)
            for j in range(TOP):
                code = jnp.where(key[j : j + 1, :] == clusters, labels[j : j + 1, :], code)
            filled = code > 0.0
            rank = jnp.dot(filled.astype(BF16), before, preferred_element_type=F32)
            rank = jnp.where(filled, rank, -1.0)
            rank_ref[s] = rank
            code_rows = spread(code)

            def rows_at(place):
                match = spread(place) == places
                label = jnp.where(match, code_rows, 0.0).astype(BF16)
                return match.astype(BF16).reshape(-1, QUERIES), label.reshape(-1, QUERIES)

            pick, label = rows_at(rank)
            found = jnp.dot(
                pick,
                q_ref[s // 2, s % 2 * QUERIES : (s % 2 + 1) * QUERIES, :],
                preferred_element_type=F32,
            ).reshape(LOCAL, 8, WIDTH)
            target_ref[:, s * 8 : s * 8 + 8, :] = jnp.dot(
                label, ones, preferred_element_type=F32
            ).reshape(LOCAL, 8, LEAF)
            pick, label = rows_at(late_places(rank, i))
            extra.append(pick)
            extra_target.append(label)
            if i % 2 == 1:
                pair = jnp.concatenate([previous, found], axis=1).astype(BF16)
                row = first_row + (s - 1) * 8
                x_ref[:, row : row + 16, :] = pair
            previous = found
        late.append(
            sum(
                jnp.dot(
                    jnp.concatenate(extra[2 * n : 2 * n + 2], axis=1),
                    q_ref[2 * group + n, : 2 * QUERIES, :],
                    preferred_element_type=F32,
                )
                for n in range(2)
            ).reshape(LOCAL, 8, WIDTH)
        )
        label = sum(jnp.dot(e, ones, preferred_element_type=F32) for e in extra_target)
        row = 32 * groups + group * 8
        target_ref[:, row : row + 8, :] = label.reshape(LOCAL, 8, LEAF)
    if groups == 1:
        late.append(jnp.zeros_like(late[0]))
        target_ref[:, 40:48, :] = jnp.zeros((LOCAL, 8, LEAF), F32)
    row = first_row + 32 * groups
    x_ref[:, row : row + 16, :] = jnp.concatenate(late, axis=1).astype(BF16)


def residuals(groups, x_ref, w_ref, target_ref, r_ref, grad_ref, first_row, prepare=None):
    rows = bucket_rows(groups)
    leaves = lax.broadcasted_iota(jnp.int32, (rows, LEAF), 1).astype(F32) + 1.0

    @pl.loop(0, LOCAL, step=UNROLL)
    def _(first):
        steps = [first + n for n in range(UNROLL)]
        if prepare is not None:
            prepare(first)
        logits = [
            lax.dot_general(
                x_ref[c, first_row : first_row + rows, :],
                w_ref[c],
                (((1,), (1,)), ((), ())),
                preferred_element_type=F32,
            )
            for c in steps
        ]
        found = []
        for c, value in zip(steps, logits):
            label = (target_ref[c] == leaves).astype(F32)
            found.append((jax.nn.sigmoid(value) - label).astype(BF16))
            r_ref[c, first_row : first_row + rows, :] = found[-1]
        if grad_ref is not None:
            for c, residual in zip(steps, found):
                grad_ref[c] = jnp.dot(residual, w_ref[c], preferred_element_type=F32)


def put_back(groups, group, rank_ref, grad_ref, p_ref, p_hbm, sem):
    places = row_places()
    row = 32 * groups + group * 8
    far = grad_ref[:, row : row + 8, :].reshape(LOCAL * 8, WIDTH).astype(BF16)
    for i in range(HALF):
        s = group * HALF + i
        rank = rank_ref[s]
        picks = [
            (spread(place) == places).astype(BF16).reshape(-1, QUERIES)
            for place in (rank, late_places(rank, i))
        ]
        near = grad_ref[:, s * 8 : s * 8 + 8, :].reshape(LOCAL * 8, WIDTH).astype(BF16)
        part = pl.ds(i * QUERIES, QUERIES)
        p_ref[group, part, :] = lax.dot_general(
            jnp.concatenate(picks, axis=0),
            jnp.concatenate([near, far], axis=0),
            (((0,), (0,)), ((), ())),
            preferred_element_type=F32,
        ).astype(BF16)
        pltpu.make_async_copy(p_ref.at[group, part], p_hbm.at[part], sem).start()
    return pltpu.make_async_copy(p_ref.at[group], p_hbm, sem)


def chunk_kernel(groups, first, me_ref, *refs):
    stacks, refs = refs[: 2 * groups], refs[2 * groups :]
    w_hbm, x_hbm, r_hbm, p_hbm, refs = refs[0], refs[1], refs[2], refs[3 : 3 + groups], refs[3 + groups :]
    if first:
        rounded_hbm, wide_ref, refs = refs[0], refs[1], refs[2:]
    q_ref, w_ref, x_ref, r_ref, p_ref, target_ref, grad_ref, rank_ref, sems = refs
    copies = [
        pltpu.make_async_copy(stack, q_ref.at[n], sems.at[n]) for n, stack in enumerate(stacks)
    ]

    def weight_copy(start, count):
        part = pl.ds(start, count)
        target = wide_ref if first else w_ref
        return pltpu.make_async_copy(w_hbm.at[part], target.at[part], sems.at[9 + start // count])

    for copy in copies:
        copy.start()
    x_copy = pltpu.make_async_copy(x_ref, x_hbm, sems.at[4])
    r_copy = pltpu.make_async_copy(r_ref, r_hbm, sems.at[5])
    copies[0].wait()
    if first:
        for start in range(0, LOCAL, UNROLL):
            weight_copy(start, UNROLL).start()
    else:
        weight_copy(0, LOCAL).start()
    select(groups, me_ref[0].astype(F32), q_ref, copies, x_ref, target_ref, rank_ref, 0)
    x_copy.start()

    def round_weights(start):
        weight_copy(start, UNROLL).wait()
        for n in range(UNROLL):
            w_ref[start + n] = wide_ref[start + n].astype(BF16)

    if not first:
        weight_copy(0, LOCAL).wait()
    residuals(
        groups, x_ref, w_ref, target_ref, r_ref, grad_ref, 0, round_weights if first else None
    )
    if first:
        rounded_copy = pltpu.make_async_copy(w_ref, rounded_hbm, sems.at[8])
        rounded_copy.start()
    r_copy.start()
    p_copies = []
    for group in range(groups):
        p_copies.append(
            put_back(groups, group, rank_ref, grad_ref, p_ref, p_hbm[group], sems.at[6 + group])
        )
    if first:
        rounded_copy.wait()
    for copy in [x_copy, r_copy] + p_copies:
        copy.wait()


def scratch(groups, rows):
    return [
        pltpu.VMEM((2 * groups, STACK, WIDTH), BF16),
        pltpu.VMEM((LOCAL, LEAF, WIDTH), BF16),
        pltpu.VMEM((LOCAL, rows, WIDTH), BF16),
        pltpu.VMEM((LOCAL, rows, LEAF), BF16),
    ]


def options(flops, traffic):
    return dict(
        compiler_params=pltpu.CompilerParams(vmem_limit_bytes=60 * MIB),
        cost_estimate=pl.CostEstimate(flops=flops, bytes_accessed=traffic, transcendentals=0),
    )


ANYWHERE = pl.BlockSpec(memory_space=pl.ANY)
SCALAR = pl.BlockSpec(memory_space=pltpu.SMEM)


def chunk(me, stacks, weights):
    groups = len(stacks) // 2
    rows = bucket_rows(groups)
    first = weights.dtype == F32
    shape = (LOCAL, LEAF, WIDTH)
    return pl.pallas_call(
        functools.partial(chunk_kernel, groups, first),
        out_shape=(
            jax.ShapeDtypeStruct((LOCAL, rows, WIDTH), BF16),
            jax.ShapeDtypeStruct((LOCAL, rows, LEAF), BF16),
        )
        + (jax.ShapeDtypeStruct((CHUNK, WIDTH), BF16),) * groups
        + (jax.ShapeDtypeStruct(shape, BF16),) * first,
        in_specs=[SCALAR] + [ANYWHERE] * (len(stacks) + 1),
        out_specs=(ANYWHERE,) * (2 + groups + first),
        scratch_shapes=[pltpu.VMEM(shape, F32)] * first
        + scratch(groups, rows)
        + [
            pltpu.VMEM((groups, CHUNK, WIDTH), BF16),
            pltpu.VMEM((LOCAL, rows, LEAF), F32),
            pltpu.VMEM((LOCAL, rows, WIDTH), F32),
            pltpu.VMEM((groups * HALF, LOCAL, QUERIES), F32),
            pltpu.SemaphoreType.DMA((13,)),
        ],
        **options(8 * groups * 10**9, 20 * groups * 10**6),
    )(me, *stacks, weights)


def last_kernel(starts, me_ref, group_ref, *refs):
    stacks, w_hbm, xs, rs, refs = refs[:2], refs[2], refs[3:7], refs[7:11], refs[11:]
    (p_hbm, own, up_a, up_b, far_a, far_b, down_a, down_b), refs = refs[:8], refs[8:]
    q_ref, w_ref, x_ref, r_ref, g_ref, p_ref, target_ref, grad_ref, total_ref, rank_ref, sems = refs
    copies = [
        pltpu.make_async_copy(stack, q_ref.at[n], sems.at[n]) for n, stack in enumerate(stacks)
    ]
    weight_copy = pltpu.make_async_copy(w_hbm, w_ref, sems.at[2])
    older = []
    for quarter in range(4):
        part = pl.ds(8 * quarter, 8)
        for n in range(4):
            rows = pl.ds(starts[n], xs[n].shape[1])
            place = 22 + 8 * quarter + 2 * n
            older.append(
                pltpu.make_async_copy(xs[n].at[part], x_ref.at[part, rows], sems.at[place])
            )
            older.append(
                pltpu.make_async_copy(rs[n].at[part], r_ref.at[part, rows], sems.at[place + 1])
            )
    for copy in copies + [weight_copy] + older[:16]:
        copy.start()
    copies[0].wait()
    first_row = starts[4]
    select(1, me_ref[0].astype(F32), q_ref, copies, x_ref, target_ref, rank_ref, first_row)
    for copy in older[16:]:
        copy.start()
    weight_copy.wait()
    residuals(1, x_ref, w_ref, target_ref, r_ref, grad_ref, first_row)
    p_copy = put_back(1, 0, rank_ref, grad_ref, p_ref, p_hbm, sems.at[12])
    group = group_ref[0]
    targets = (
        (own.at[pl.ds(0, 16)], own.at[pl.ds(16, 16)]),
        (up_a, up_b),
        (far_a, far_b),
        (down_a, down_b),
    )
    grad_copies = []
    for quarter in range(4):
        for copy in older[8 * quarter : 8 * quarter + 8]:
            copy.wait()

        @pl.loop(0, 8, step=4)
        def _(first):
            for n in range(4):
                c = quarter * 8 + first + n
                total_ref[n] = lax.dot_general(
                    r_ref[c], x_ref[c], (((0,), (0,)), ((), ())), preferred_element_type=F32
                )
            for n in range(4):
                for away in range(4):
                    start = pl.multiple_of(((group + away) % 4) * 32, 32)
                    place = 2 * away + quarter // 2
                    g_ref[place, quarter % 2 * 8 + first + n] = total_ref[
                        n, pl.ds(start, 32), :
                    ].astype(BF16)

        for away in range(4):
            part = pl.ds(quarter % 2 * 8, 8)
            copy = pltpu.make_async_copy(
                g_ref.at[2 * away + quarter // 2, part],
                targets[away][quarter // 2].at[part],
                sems.at[54 + 4 * quarter + away],
            )
            copy.start()
            grad_copies.append(copy)
    for copy in [p_copy] + grad_copies:
        copy.wait()


def last_chunk(me, group, stacks, weights, xs, rs):
    rows = bucket_rows(1)
    starts = [0]
    for x in xs:
        starts.append(starts[-1] + x.shape[1])
    all_rows = starts[-1] + rows
    whole = jax.ShapeDtypeStruct((LOCAL, 32, WIDTH), BF16)
    half = jax.ShapeDtypeStruct((16, 32, WIDTH), BF16)
    return pl.pallas_call(
        functools.partial(last_kernel, starts),
        out_shape=(jax.ShapeDtypeStruct((CHUNK, WIDTH), BF16),) + (whole,) + (half,) * 6,
        in_specs=[SCALAR] * 2 + [ANYWHERE] * 11,
        out_specs=(ANYWHERE,) * 8,
        scratch_shapes=scratch(1, all_rows)
        + [
            pltpu.VMEM((8, 16, 32, WIDTH), BF16),
            pltpu.VMEM((1, CHUNK, WIDTH), BF16),
            pltpu.VMEM((LOCAL, rows, LEAF), F32),
            pltpu.VMEM((LOCAL, rows, WIDTH), F32),
            pltpu.VMEM((4, LEAF, WIDTH), F32),
            pltpu.VMEM((HALF, LOCAL, QUERIES), F32),
            pltpu.SemaphoreType.DMA((70,)),
        ],
        **options(8 * 10**9, 40 * 10**6),
    )(me, group, *stacks, weights, *xs, *rs)


def class_sum_kernel(own_ref, low_refs, high_refs, out_hbm, out_ref, sems):
    copies = []
    for n in range(4):
        part = slice(8 * n, 8 * n + 8)
        half = slice(8 * (n % 2), 8 * (n % 2) + 8)
        out_ref[part] = add(own_ref[part], *[ref[half] for ref in (low_refs, high_refs)[n // 2]])
        copies.append(pltpu.make_async_copy(out_ref.at[part], out_hbm.at[part], sems.at[n]))
        copies[-1].start()
    for copy in copies:
        copy.wait()


def class_sum(own, low, high):
    in_vmem = pl.BlockSpec(memory_space=pltpu.VMEM)
    return pl.pallas_call(
        class_sum_kernel,
        out_shape=jax.ShapeDtypeStruct((LOCAL, 32, WIDTH), F32),
        in_specs=[in_vmem, (in_vmem,) * 2, (in_vmem,) * 2],
        out_specs=ANYWHERE,
        scratch_shapes=[pltpu.VMEM((LOCAL, 32, WIDTH), F32), pltpu.SemaphoreType.DMA((4,))],
        compiler_params=pltpu.CompilerParams(vmem_limit_bytes=24 * MIB),
        cost_estimate=pl.CostEstimate(flops=10**6, bytes_accessed=8 * 10**6, transcendentals=0),
    )(own, low, high)


def body(queries, classifier, routed, positives, cluster_slot):
    me = lax.axis_index("al").astype(jnp.int32).reshape(1)
    group = lax.axis_index("pb").astype(jnp.int32).reshape(1)
    payload = payload_of(queries, routed, positives, cluster_slot)

    up, down = send(payload, NEAR_UP), send(payload, NEAR_DOWN)
    cut = 144
    across = jnp.concatenate([send(up[:cut], NEAR_UP), send(down[cut:], NEAR_DOWN)], axis=0)

    def stack(first, second):
        return jnp.concatenate(
            [first[:QUERIES], second[:QUERIES], first[QUERIES:], second[QUERIES:]], axis=0
        )

    def swap(stacks):
        return [send(s, SWAP) for s in stacks]

    home = [stack(payload, up), stack(down, across)]
    home = lax.optimization_barrier(home)
    near_half = [send(home[0], FAR_UP), send(home[1], FAR_DOWN)]
    x, r, p_home, weights = chunk(me, home, classifier)
    xs, rs = [x], [r]
    near_half, home, xs = lax.optimization_barrier((near_half, home, xs))
    far_half = [send(home[0], FAR_DOWN), send(home[1], FAR_UP)]
    x, r, p_near, q_home = chunk(me, near_half + swap(home), weights)
    near_half, x, r = lax.optimization_barrier((near_half, x, r))
    xs.append(x), rs.append(r)
    last = [send(near_half[0], FAR_UP), send(near_half[1], FAR_DOWN)]
    x, r, p_far, q_near = chunk(me, far_half + swap(near_half), weights)
    last, x, r = lax.optimization_barrier((last, x, r))
    xs.append(x), rs.append(r)

    def two_cores(mine, other):
        total = add(mine, send(other, SWAP)).astype(BF16)
        return total[: CHUNK // 2], total[CHUNK // 2 :]

    x, r, p_last, q_far = chunk(me, last + swap(far_half), weights)
    xs.append(x), rs.append(r)
    outs = last_chunk(me, group, swap(last), weights, xs, rs)
    q_last, own, next_up_a, next_up_b, opposite_a, opposite_b, next_down_a, next_down_b = outs

    far_a, far_b = two_cores(p_last, q_last)
    arrived = lax.optimization_barrier(
        (
            send_z(opposite_a, Z_UP),
            send_z(opposite_b, Z_DOWN),
            send(far_a, FAR_UP),
            send(far_b, FAR_DOWN),
        )
    )
    class_below, class_above, from_low, from_high = arrived

    up_a, down_b = two_cores(p_near, q_near)
    down_a, up_b = two_cores(p_far, q_far)
    sends = (
        add(next_up_a, class_below).astype(BF16),
        add(next_down_b, class_above).astype(BF16),
        jnp.concatenate([add(down_a, from_low).astype(BF16), down_b]),
        jnp.concatenate([up_a, add(up_b, from_high).astype(BF16)]),
        next_up_b,
        next_down_a,
    )
    class_to_up, class_to_down, to_up, to_down, *rest = lax.optimization_barrier(sends)
    arrived = lax.optimization_barrier(
        (
            send_z(class_to_up, Z_UP),
            send_z(class_to_down, Z_DOWN),
            send(to_up, FAR_UP),
            send(to_down, FAR_DOWN),
            *rest,
        )
    )
    sum_below_a, sum_above_b, from_low, from_high, next_up_b, next_down_a = arrived

    home_a, home_b = two_cores(p_home, q_home)
    cut = CHUNK // 2
    first = add(home_a, from_low[:cut], from_high[:cut])
    second = add(home_b, from_low[cut:], from_high[cut:])
    mid = QUERIES // 2

    def halves(total):
        total = total.astype(BF16)
        return total[:mid], total[mid:]

    below_b, above_a = send_z(next_up_b, Z_UP), send_z(next_down_a, Z_DOWN)
    up, down, across = halves(first[QUERIES:]), halves(second[:QUERIES]), halves(second[QUERIES:])
    low = send(jnp.concatenate([across[0], down[1]]), NEAR_UP)
    high = send(jnp.concatenate([up[0], across[1]]), NEAR_DOWN)
    low_sum = send(add(down[0], low[:mid]).astype(BF16), NEAR_UP)
    high_sum = send(add(up[1], high[mid:]).astype(BF16), NEAR_DOWN)
    query_grad = jnp.concatenate(
        [add(first[:mid], low_sum, high[:mid]), add(first[mid:QUERIES], low[mid:], high_sum)],
        axis=0,
    )
    below_b, above_a, query_grad = lax.optimization_barrier((below_b, above_a, query_grad))
    class_grad = class_sum(own, (sum_below_a, above_a), (below_b, sum_above_b))
    return query_grad, class_grad


def solution(mesh):
    return jax.shard_map(
        body,
        mesh=mesh,
        in_specs=(
            P(("pb", "al"), None),
            P("al", None, None),
            P(("pb", "al"), None),
            P(("pb", "al"), None),
            P(),
        ),
        out_specs=(P(("pb", "al"), None), P("al", "pb", None)),
        check_vma=False,
    )
```

```python
import functools

import jax
import jax.numpy as jnp
from jax import lax
from jax.experimental import pallas as pl
from jax.experimental.pallas import tpu as pltpu
from jax.sharding import PartitionSpec as P

F32 = jnp.float32
BF16 = jnp.bfloat16
SIDE = 4
QUERIES = 256
TOP = 16
WIDTH = 768
LEAF = 128
LOCAL = 32
HALF = 4
PAYLOAD = QUERIES + TOP
CHUNK = HALF * QUERIES
STACK = 2 * PAYLOAD
MIB = 1 << 20
UNROLL = 8


def al_index(x, y, core):
    return ((x % SIDE) * SIDE + y % SIDE) * 2 + core


def shift(first, second):
    pairs = []
    for x in range(SIDE):
        for y in range(SIDE):
            pairs.append((al_index(x, y, 0), al_index(x + first[0], y + first[1], 0)))
            pairs.append((al_index(x, y, 1), al_index(x + second[0], y + second[1], 1)))
    return pairs


NEAR_UP, NEAR_DOWN = shift((1, 0), (0, 1)), shift((-1, 0), (0, -1))
FAR_UP, FAR_DOWN = shift((0, 1), (1, 0)), shift((0, -1), (-1, 0))
SWAP = [(i, i ^ 1) for i in range(2 * SIDE * SIDE)]
Z_UP = [(i, (i + 1) % SIDE) for i in range(SIDE)]
Z_DOWN = [(i, (i - 1) % SIDE) for i in range(SIDE)]


def send(value, pairs):
    return lax.ppermute(value, "al", pairs)


def send_z(value, pairs):
    return lax.ppermute(value, "pb", pairs)


def add(first, *others):
    total = first.astype(F32)
    for other in others:
        total = total + other.astype(F32)
    return total


def payload_kernel(q_ref, routed_ref, positives_ref, table_ref, out_ref):
    out_ref[:QUERIES, :] = q_ref[...]
    slots = table_ref[...]
    table = jnp.concatenate([slots // LOCAL, slots % LOCAL], axis=0).astype(F32).astype(BF16)
    lanes = lax.broadcasted_iota(jnp.int32, (128, QUERIES), 0)
    highs = lax.broadcasted_iota(jnp.int32, (8, QUERIES), 0)
    ids = routed_ref[...]
    rows = []
    for j in range(TOP):
        one = ids[j : j + 1, :]
        low = (one % 128 == lanes).astype(F32).astype(BF16)
        found = jnp.dot(table, low, preferred_element_type=F32)
        high = one // 128 == highs
        rows.append(
            jnp.concatenate(
                [
                    jnp.sum(jnp.where(high, found[:8], 0.0), axis=0, keepdims=True),
                    jnp.sum(jnp.where(high, found[8:], 0.0), axis=0, keepdims=True),
                ],
                axis=1,
            )
        )
    found = jnp.concatenate(rows, axis=0)
    labels = positives_ref[...].astype(F32)
    out_ref[QUERIES:, :] = jnp.concatenate([found, labels], axis=1).astype(BF16)


def payload_of(queries, routed, positives, cluster_slot):
    return pl.pallas_call(
        payload_kernel,
        out_shape=jax.ShapeDtypeStruct((PAYLOAD, WIDTH), BF16),
        cost_estimate=pl.CostEstimate(flops=10**8, bytes_accessed=10**6, transcendentals=0),
    )(queries, routed.T, positives.T, cluster_slot.reshape(8, 128))


def bucket_rows(groups):
    return -(-40 * groups // 16) * 16


def spread(value):
    return jnp.broadcast_to(value[:, None, :], (LOCAL, 8, QUERIES))


def late_places(rank, i):
    return jnp.where(rank >= 8.0, rank - 8.0 + 2.0 * i, -1.0)


def row_places():
    return lax.broadcasted_iota(jnp.int32, (LOCAL, 8, QUERIES), 1).astype(F32)


def select(groups, me, q_ref, copies, x_ref, target_ref, rank_ref, first_row):
    before = (
        lax.broadcasted_iota(jnp.int32, (QUERIES, QUERIES), 0)
        < lax.broadcasted_iota(jnp.int32, (QUERIES, QUERIES), 1)
    ).astype(BF16)
    clusters = lax.broadcasted_iota(jnp.int32, (LOCAL, QUERIES), 0).astype(F32)
    places = row_places()
    ones = jnp.ones((QUERIES, LEAF), BF16)
    late = []
    for group in range(groups):
        extra = []
        extra_target = []
        for i in range(HALF):
            s = group * HALF + i
            if s % 2 == 0 and s > 0:
                copies[s // 2].wait()
            start = 2 * QUERIES + s % 2 * TOP
            meta = q_ref[s // 2, start : start + TOP, :].astype(F32)
            key = jnp.where(meta[:, :QUERIES] == me, meta[:, QUERIES : 2 * QUERIES], -1.0)
            labels = meta[:, 2 * QUERIES :] + 1.0
            code = jnp.zeros((LOCAL, QUERIES), F32)
            for j in range(TOP):
                code = jnp.where(key[j : j + 1, :] == clusters, labels[j : j + 1, :], code)
            filled = code > 0.0
            rank = jnp.dot(filled.astype(BF16), before, preferred_element_type=F32)
            rank = jnp.where(filled, rank, -1.0)
            rank_ref[s] = rank
            code_rows = spread(code)

            def rows_at(place):
                match = spread(place) == places
                label = jnp.where(match, code_rows, 0.0).astype(BF16)
                return match.astype(BF16).reshape(-1, QUERIES), label.reshape(-1, QUERIES)

            pick, label = rows_at(rank)
            found = jnp.dot(
                pick,
                q_ref[s // 2, s % 2 * QUERIES : (s % 2 + 1) * QUERIES, :],
                preferred_element_type=F32,
            ).reshape(LOCAL, 8, WIDTH)
            target_ref[:, s * 8 : s * 8 + 8, :] = jnp.dot(
                label, ones, preferred_element_type=F32
            ).reshape(LOCAL, 8, LEAF)
            pick, label = rows_at(late_places(rank, i))
            extra.append(pick)
            extra_target.append(label)
            if i % 2 == 1:
                pair = jnp.concatenate([previous, found], axis=1).astype(BF16)
                row = first_row + (s - 1) * 8
                x_ref[:, row : row + 16, :] = pair
            previous = found
        late.append(
            sum(
                jnp.dot(
                    jnp.concatenate(extra[2 * n : 2 * n + 2], axis=1),
                    q_ref[2 * group + n, : 2 * QUERIES, :],
                    preferred_element_type=F32,
                )
                for n in range(2)
            ).reshape(LOCAL, 8, WIDTH)
        )
        label = sum(jnp.dot(e, ones, preferred_element_type=F32) for e in extra_target)
        row = 32 * groups + group * 8
        target_ref[:, row : row + 8, :] = label.reshape(LOCAL, 8, LEAF)
    if groups == 1:
        late.append(jnp.zeros_like(late[0]))
        target_ref[:, 40:48, :] = jnp.zeros((LOCAL, 8, LEAF), F32)
    row = first_row + 32 * groups
    x_ref[:, row : row + 16, :] = jnp.concatenate(late, axis=1).astype(BF16)


def residuals(groups, x_ref, w_ref, target_ref, r_ref, grad_ref, first_row, prepare=None):
    rows = bucket_rows(groups)
    leaves = lax.broadcasted_iota(jnp.int32, (rows, LEAF), 1).astype(F32) + 1.0

    @pl.loop(0, LOCAL, step=UNROLL)
    def _(first):
        steps = [first + n for n in range(UNROLL)]
        if prepare is not None:
            prepare(first)
        logits = [
            lax.dot_general(
                x_ref[c, first_row : first_row + rows, :],
                w_ref[c],
                (((1,), (1,)), ((), ())),
                preferred_element_type=F32,
            )
            for c in steps
        ]
        found = []
        for c, value in zip(steps, logits):
            label = (target_ref[c] == leaves).astype(F32)
            found.append((jax.nn.sigmoid(value) - label).astype(BF16))
            r_ref[c, first_row : first_row + rows, :] = found[-1]
        if grad_ref is not None:
            for c, residual in zip(steps, found):
                grad_ref[c] = jnp.dot(residual, w_ref[c], preferred_element_type=F32)


def put_back(groups, group, rank_ref, grad_ref, p_ref, p_hbm, sem):
    places = row_places()
    row = 32 * groups + group * 8
    far = grad_ref[:, row : row + 8, :].reshape(LOCAL * 8, WIDTH).astype(BF16)
    for i in range(HALF):
        s = group * HALF + i
        rank = rank_ref[s]
        picks = [
            (spread(place) == places).astype(BF16).reshape(-1, QUERIES)
            for place in (rank, late_places(rank, i))
        ]
        near = grad_ref[:, s * 8 : s * 8 + 8, :].reshape(LOCAL * 8, WIDTH).astype(BF16)
        part = pl.ds(i * QUERIES, QUERIES)
        p_ref[group, part, :] = lax.dot_general(
            jnp.concatenate(picks, axis=0),
            jnp.concatenate([near, far], axis=0),
            (((0,), (0,)), ((), ())),
            preferred_element_type=F32,
        ).astype(BF16)
        pltpu.make_async_copy(p_ref.at[group, part], p_hbm.at[part], sem).start()
    return pltpu.make_async_copy(p_ref.at[group], p_hbm, sem)


def chunk_kernel(groups, first, me_ref, *refs):
    stacks, refs = refs[: 2 * groups], refs[2 * groups :]
    w_hbm, x_hbm, r_hbm, p_hbm, refs = refs[0], refs[1], refs[2], refs[3 : 3 + groups], refs[3 + groups :]
    if first:
        rounded_hbm, wide_ref, refs = refs[0], refs[1], refs[2:]
    q_ref, w_ref, x_ref, r_ref, p_ref, target_ref, grad_ref, rank_ref, sems = refs
    copies = [
        pltpu.make_async_copy(stack, q_ref.at[n], sems.at[n]) for n, stack in enumerate(stacks)
    ]

    def weight_copy(start, count):
        part = pl.ds(start, count)
        target = wide_ref if first else w_ref
        return pltpu.make_async_copy(w_hbm.at[part], target.at[part], sems.at[9 + start // count])

    for copy in copies:
        copy.start()
    x_copy = pltpu.make_async_copy(x_ref, x_hbm, sems.at[4])
    r_copy = pltpu.make_async_copy(r_ref, r_hbm, sems.at[5])
    if first:
        for start in range(0, LOCAL, UNROLL):
            weight_copy(start, UNROLL).start()
    copies[0].wait()
    if not first:
        weight_copy(0, LOCAL).start()
    select(groups, me_ref[0].astype(F32), q_ref, copies, x_ref, target_ref, rank_ref, 0)
    x_copy.start()

    def round_weights(start):
        weight_copy(start, UNROLL).wait()
        for n in range(UNROLL):
            w_ref[start + n] = wide_ref[start + n].astype(BF16)

    if not first:
        weight_copy(0, LOCAL).wait()
    residuals(
        groups, x_ref, w_ref, target_ref, r_ref, grad_ref, 0, round_weights if first else None
    )
    if first:
        rounded_copy = pltpu.make_async_copy(w_ref, rounded_hbm, sems.at[8])
        rounded_copy.start()
    r_copy.start()
    p_copies = []
    for group in range(groups):
        p_copies.append(
            put_back(groups, group, rank_ref, grad_ref, p_ref, p_hbm[group], sems.at[6 + group])
        )
    if first:
        rounded_copy.wait()
    for copy in [x_copy, r_copy] + p_copies:
        copy.wait()


def scratch(groups, rows):
    return [
        pltpu.VMEM((2 * groups, STACK, WIDTH), BF16),
        pltpu.VMEM((LOCAL, LEAF, WIDTH), BF16),
        pltpu.VMEM((LOCAL, rows, WIDTH), BF16),
        pltpu.VMEM((LOCAL, rows, LEAF), BF16),
    ]


def options(flops, traffic):
    return dict(
        compiler_params=pltpu.CompilerParams(vmem_limit_bytes=60 * MIB),
        cost_estimate=pl.CostEstimate(flops=flops, bytes_accessed=traffic, transcendentals=0),
    )


ANYWHERE = pl.BlockSpec(memory_space=pl.ANY)
SCALAR = pl.BlockSpec(memory_space=pltpu.SMEM)


def chunk(me, stacks, weights):
    groups = len(stacks) // 2
    rows = bucket_rows(groups)
    first = weights.dtype == F32
    shape = (LOCAL, LEAF, WIDTH)
    return pl.pallas_call(
        functools.partial(chunk_kernel, groups, first),
        out_shape=(
            jax.ShapeDtypeStruct((LOCAL, rows, WIDTH), BF16),
            jax.ShapeDtypeStruct((LOCAL, rows, LEAF), BF16),
        )
        + (jax.ShapeDtypeStruct((CHUNK, WIDTH), BF16),) * groups
        + (jax.ShapeDtypeStruct(shape, BF16),) * first,
        in_specs=[SCALAR] + [ANYWHERE] * (len(stacks) + 1),
        out_specs=(ANYWHERE,) * (2 + groups + first),
        scratch_shapes=[pltpu.VMEM(shape, F32)] * first
        + scratch(groups, rows)
        + [
            pltpu.VMEM((groups, CHUNK, WIDTH), BF16),
            pltpu.VMEM((LOCAL, rows, LEAF), F32),
            pltpu.VMEM((LOCAL, rows, WIDTH), F32),
            pltpu.VMEM((groups * HALF, LOCAL, QUERIES), F32),
            pltpu.SemaphoreType.DMA((13,)),
        ],
        **options(8 * groups * 10**9, 20 * groups * 10**6),
    )(me, *stacks, weights)


def last_kernel(starts, me_ref, group_ref, *refs):
    stacks, w_hbm, xs, rs, refs = refs[:2], refs[2], refs[3:7], refs[7:11], refs[11:]
    (p_hbm, own, up_a, up_b, far_a, far_b, down_a, down_b), refs = refs[:8], refs[8:]
    q_ref, w_ref, x_ref, r_ref, g_ref, p_ref, target_ref, grad_ref, total_ref, rank_ref, sems = refs
    copies = [
        pltpu.make_async_copy(stack, q_ref.at[n], sems.at[n]) for n, stack in enumerate(stacks)
    ]
    weight_copy = pltpu.make_async_copy(w_hbm, w_ref, sems.at[2])
    older = []
    for quarter in range(4):
        part = pl.ds(8 * quarter, 8)
        for n in range(4):
            rows = pl.ds(starts[n], xs[n].shape[1])
            place = 22 + 8 * quarter + 2 * n
            older.append(
                pltpu.make_async_copy(xs[n].at[part], x_ref.at[part, rows], sems.at[place])
            )
            older.append(
                pltpu.make_async_copy(rs[n].at[part], r_ref.at[part, rows], sems.at[place + 1])
            )
    for copy in copies + [weight_copy] + older[:16]:
        copy.start()
    copies[0].wait()
    first_row = starts[4]
    select(1, me_ref[0].astype(F32), q_ref, copies, x_ref, target_ref, rank_ref, first_row)
    for copy in older[16:]:
        copy.start()
    weight_copy.wait()
    residuals(1, x_ref, w_ref, target_ref, r_ref, grad_ref, first_row)
    p_copy = put_back(1, 0, rank_ref, grad_ref, p_ref, p_hbm, sems.at[12])
    group = group_ref[0]
    targets = (
        (own.at[pl.ds(0, 16)], own.at[pl.ds(16, 16)]),
        (up_a, up_b),
        (far_a, far_b),
        (down_a, down_b),
    )
    grad_copies = []
    for quarter in range(4):
        for copy in older[8 * quarter : 8 * quarter + 8]:
            copy.wait()

        @pl.loop(0, 8, step=4)
        def _(first):
            for n in range(4):
                c = quarter * 8 + first + n
                total_ref[n] = lax.dot_general(
                    r_ref[c], x_ref[c], (((0,), (0,)), ((), ())), preferred_element_type=F32
                )
            for n in range(4):
                for away in range(4):
                    start = pl.multiple_of(((group + away) % 4) * 32, 32)
                    place = 2 * away + quarter // 2
                    g_ref[place, quarter % 2 * 8 + first + n] = total_ref[
                        n, pl.ds(start, 32), :
                    ].astype(BF16)

        for away in range(4):
            part = pl.ds(quarter % 2 * 8, 8)
            copy = pltpu.make_async_copy(
                g_ref.at[2 * away + quarter // 2, part],
                targets[away][quarter // 2].at[part],
                sems.at[54 + 4 * quarter + away],
            )
            copy.start()
            grad_copies.append(copy)
    for copy in [p_copy] + grad_copies:
        copy.wait()


def last_chunk(me, group, stacks, weights, xs, rs):
    rows = bucket_rows(1)
    starts = [0]
    for x in xs:
        starts.append(starts[-1] + x.shape[1])
    all_rows = starts[-1] + rows
    whole = jax.ShapeDtypeStruct((LOCAL, 32, WIDTH), BF16)
    half = jax.ShapeDtypeStruct((16, 32, WIDTH), BF16)
    return pl.pallas_call(
        functools.partial(last_kernel, starts),
        out_shape=(jax.ShapeDtypeStruct((CHUNK, WIDTH), BF16),) + (whole,) + (half,) * 6,
        in_specs=[SCALAR] * 2 + [ANYWHERE] * 11,
        out_specs=(ANYWHERE,) * 8,
        scratch_shapes=scratch(1, all_rows)
        + [
            pltpu.VMEM((8, 16, 32, WIDTH), BF16),
            pltpu.VMEM((1, CHUNK, WIDTH), BF16),
            pltpu.VMEM((LOCAL, rows, LEAF), F32),
            pltpu.VMEM((LOCAL, rows, WIDTH), F32),
            pltpu.VMEM((4, LEAF, WIDTH), F32),
            pltpu.VMEM((HALF, LOCAL, QUERIES), F32),
            pltpu.SemaphoreType.DMA((70,)),
        ],
        **options(8 * 10**9, 40 * 10**6),
    )(me, group, *stacks, weights, *xs, *rs)


def class_sum_kernel(own_ref, low_refs, high_refs, out_hbm, out_ref, sems):
    copies = []
    for n in range(8):
        part = slice(4 * n, 4 * n + 4)
        half = slice(4 * (n % 4), 4 * (n % 4) + 4)
        out_ref[part] = add(own_ref[part], *[ref[half] for ref in (low_refs, high_refs)[n // 4]])
        copies.append(pltpu.make_async_copy(out_ref.at[part], out_hbm.at[part], sems.at[n]))
        copies[-1].start()
    for copy in copies:
        copy.wait()


def class_sum(own, low, high):
    in_vmem = pl.BlockSpec(memory_space=pltpu.VMEM)
    return pl.pallas_call(
        class_sum_kernel,
        out_shape=jax.ShapeDtypeStruct((LOCAL, 32, WIDTH), F32),
        in_specs=[in_vmem, (in_vmem,) * 2, (in_vmem,) * 2],
        out_specs=ANYWHERE,
        scratch_shapes=[pltpu.VMEM((LOCAL, 32, WIDTH), F32), pltpu.SemaphoreType.DMA((8,))],
        compiler_params=pltpu.CompilerParams(vmem_limit_bytes=24 * MIB),
        cost_estimate=pl.CostEstimate(flops=10**6, bytes_accessed=8 * 10**6, transcendentals=0),
    )(own, low, high)


def body(queries, classifier, routed, positives, cluster_slot):
    me = lax.axis_index("al").astype(jnp.int32).reshape(1)
    group = lax.axis_index("pb").astype(jnp.int32).reshape(1)
    payload = payload_of(queries, routed, positives, cluster_slot)

    up, down = send(payload, NEAR_UP), send(payload, NEAR_DOWN)
    cut = 144
    across = jnp.concatenate([send(up[:cut], NEAR_UP), send(down[cut:], NEAR_DOWN)], axis=0)

    def stack(first, second):
        return jnp.concatenate(
            [first[:QUERIES], second[:QUERIES], first[QUERIES:], second[QUERIES:]], axis=0
        )

    def swap(stacks):
        return [send(s, SWAP) for s in stacks]

    home = [stack(payload, up), stack(down, across)]
    home = lax.optimization_barrier(home)
    near_half = [send(home[0], FAR_UP), send(home[1], FAR_DOWN)]
    x, r, p_home, weights = chunk(me, home, classifier)
    xs, rs = [x], [r]
    near_half, home, xs = lax.optimization_barrier((near_half, home, xs))
    far_half = [send(home[0], FAR_DOWN), send(home[1], FAR_UP)]
    x, r, p_near, q_home = chunk(me, near_half + swap(home), weights)
    near_half, x, r = lax.optimization_barrier((near_half, x, r))
    xs.append(x), rs.append(r)
    last = [send(near_half[0], FAR_UP), send(near_half[1], FAR_DOWN)]
    x, r, p_far, q_near = chunk(me, far_half + swap(near_half), weights)
    last, x, r = lax.optimization_barrier((last, x, r))
    xs.append(x), rs.append(r)

    def two_cores(mine, other):
        total = add(mine, send(other, SWAP)).astype(BF16)
        return total[: CHUNK // 2], total[CHUNK // 2 :]

    x, r, p_last, q_far = chunk(me, last + swap(far_half), weights)
    xs.append(x), rs.append(r)
    outs = last_chunk(me, group, swap(last), weights, xs, rs)
    q_last, own, next_up_a, next_up_b, opposite_a, opposite_b, next_down_a, next_down_b = outs

    far_a, far_b = two_cores(p_last, q_last)
    arrived = lax.optimization_barrier(
        (
            send_z(opposite_a, Z_UP),
            send_z(opposite_b, Z_DOWN),
            send(far_a, FAR_UP),
            send(far_b, FAR_DOWN),
        )
    )
    class_below, class_above, from_low, from_high = arrived

    up_a, down_b = two_cores(p_near, q_near)
    down_a, up_b = two_cores(p_far, q_far)
    sends = (
        add(next_up_a, class_below).astype(BF16),
        add(next_down_b, class_above).astype(BF16),
        jnp.concatenate([add(down_a, from_low).astype(BF16), down_b]),
        jnp.concatenate([up_a, add(up_b, from_high).astype(BF16)]),
        next_up_b,
        next_down_a,
    )
    class_to_up, class_to_down, to_up, to_down, *rest = lax.optimization_barrier(sends)
    arrived = lax.optimization_barrier(
        (
            send_z(class_to_up, Z_UP),
            send_z(class_to_down, Z_DOWN),
            send(to_up, FAR_UP),
            send(to_down, FAR_DOWN),
            *rest,
        )
    )
    sum_below_a, sum_above_b, from_low, from_high, next_up_b, next_down_a = arrived

    home_a, home_b = two_cores(p_home, q_home)
    cut = CHUNK // 2
    first = add(home_a, from_low[:cut], from_high[:cut])
    second = add(home_b, from_low[cut:], from_high[cut:])
    mid = QUERIES // 2

    def halves(total):
        total = total.astype(BF16)
        return total[:mid], total[mid:]

    below_b, above_a = send_z(next_up_b, Z_UP), send_z(next_down_a, Z_DOWN)
    up, down, across = halves(first[QUERIES:]), halves(second[:QUERIES]), halves(second[QUERIES:])
    low = send(jnp.concatenate([across[0], down[1]]), NEAR_UP)
    high = send(jnp.concatenate([up[0], across[1]]), NEAR_DOWN)
    low_sum = send(add(down[0], low[:mid]).astype(BF16), NEAR_UP)
    high_sum = send(add(up[1], high[mid:]).astype(BF16), NEAR_DOWN)
    query_grad = jnp.concatenate(
        [add(first[:mid], low_sum, high[:mid]), add(first[mid:QUERIES], low[mid:], high_sum)],
        axis=0,
    )
    below_b, above_a, query_grad = lax.optimization_barrier((below_b, above_a, query_grad))
    class_grad = class_sum(own, (sum_below_a, above_a), (below_b, sum_above_b))
    return query_grad, class_grad


def solution(mesh):
    return jax.shard_map(
        body,
        mesh=mesh,
        in_specs=(
            P(("pb", "al"), None),
            P("al", None, None),
            P(("pb", "al"), None),
            P(("pb", "al"), None),
            P(),
        ),
        out_specs=(P(("pb", "al"), None), P("al", "pb", None)),
        check_vma=False,
    )
```
